32 devices in a mesh: frame: 16 (over z, x, core), head: 2 (over y).
Axes of the slice: x: 2, y: 2, z: 4, core: 2. Of those that a mesh axis runs over, the one named last changes fastest.
Arguments:
- queue: bfloat16 [2048, 5120], P('frame', 'head'), may hold values from -6 to 6
- noise_block: bfloat16 [64, 5120], P(None, 'head'), may hold values from -6 to 6
- w_query: bfloat16 [5120, 768], P('frame', 'head'), may hold values from -0.078125 to 0.078125
- w_key: bfloat16 [5120, 768], P('frame', 'head'), may hold values from -0.078125 to 0.078125
- w_value: bfloat16 [5120, 768], P('frame', 'head'), may hold values from -0.078125 to 0.078125
- w_output: bfloat16 [768, 5120], P('head', 'frame'), may hold values from -1.5 to 1.5
- mod_table: float32 [64, 3, 5120], replicated, may hold values from -4 to 4
- sigma_table: float32 [65], replicated, may hold values from 0 to 1
- timestep_index: int32 [32], P('frame'), may hold values from 0 to 63
- block_position: int32 [32], P('frame'), may hold values from 0 to 4095
Outputs:
- velocity: bfloat16 [2048, 5120], P('frame', 'head')
- queue_out: bfloat16 [2048, 5120], P('frame', 'head')
The draws below stay inside these ranges and needn't reach their ends.
All inputs are finite; a program needn't handle non-finite values.
Results may differ from the reference program's by a relative error of at most 0.025.
Values may be sent and summed in bfloat16 or wider, within the bound.
A program may use at most 128 MiB of HBM per device.

```python
import math
import jax
import jax.numpy as jnp
from jax import lax

D = 5120
HEAD_SIZE = 128
HEAD_DEV = 3
REACH = 2
TOK_CH = 64
LEVELS = 64
HEADS = 6
BLOCKS = 32
TOKENS = 2048
N_HEAD = 2


def touch_ends(values, stream_key, smallest, top_value):
    longest = values.shape.index(max(values.shape))
    spots = []
    for shift in (0, 1):
        where = [jax.random.randint(jax.random.fold_in(stream_key, axis), (), 0, length) for axis, length in enumerate(values.shape)]
        where[longest] = (where[longest] + shift) % values.shape[longest]
        spots.append(tuple(where))
    return values.at[spots[0]].set(smallest).at[spots[1]].set(top_value)


def level_of(rng, dims, split, low, largest):
    def one(axis_at, shards_of):
        steps = jax.random.uniform(jax.random.fold_in(jax.random.fold_in(rng, 6), axis_at), (shards_of,), jnp.float32, low / len(split), largest / len(split))
        return jnp.repeat(jnp.exp(steps), dims[axis_at] // shards_of).reshape((-1,) + (1,) * (len(dims) - axis_at - 1))

    level = one(*split[0])
    for cut in split[1:]:
        level = level * one(*cut)
    return level


def scatter_about(rng, extent, spread, most, pieces=(), held_as=jnp.bfloat16):
    factor_of = level_of(rng, extent, pieces, -0.22, 0.18) if pieces else 1.0
    values = jax.random.normal(rng, extent, jnp.float32) * spread * factor_of
    return jnp.minimum(jnp.maximum(values, -most), most).astype(held_as)


def setup_inputs(seed: int = 0) -> dict:
    splits = jax.random.split(jax.random.key(seed), 11)
    return {
        "queue": scatter_about(splits[0], (TOKENS, D), 1.0, 6.0, ((0, 16), (1, 2))),
        "noise_block": scatter_about(splits[1], (TOK_CH, D), 1.0, 6.0, ((1, 2),)),
        "w_query": scatter_about(splits[2], (D, HEADS * HEAD_SIZE), D ** -0.5, 0.078125, ((0, 16), (1, 2))),
        "w_key": scatter_about(splits[3], (D, HEADS * HEAD_SIZE), D ** -0.5, 0.078125, ((0, 16), (1, 2))),
        "w_value": scatter_about(splits[4], (D, HEADS * HEAD_SIZE), D ** -0.5, 0.078125, ((0, 16), (1, 2))),
        "w_output": scatter_about(splits[5], (HEADS * HEAD_SIZE, D), (HEAD_SIZE // 8) ** -0.5, 1.5, ((0, 2), (1, 16))),
        "mod_table": scatter_about(splits[6], (LEVELS, 3, D), 1.0, 4.0, (), jnp.float32),
        "sigma_table": jnp.clip(jax.random.uniform(splits[7], (LEVELS + 1,), jnp.float32, 0.0, 1.0), 0.0, 1.0),
        "timestep_index": touch_ends(jax.random.randint(splits[8], (BLOCKS,), 0, LEVELS), jax.random.fold_in(splits[8], 1), 0, LEVELS - 1).astype(jnp.int32),
        "block_position": touch_ends(jax.random.randint(splits[9], (BLOCKS,), 0, 4096), jax.random.fold_in(splits[9], 1), 0, 4095).astype(jnp.int32),
    }


def norm_heads(vectors):
    return vectors * lax.rsqrt(lax.optimization_barrier(jnp.mean(vectors * vectors, axis=-1, keepdims=True)) + 1e-06)

def rotate(vectors, positions):
    half_size = vectors.shape[-1] // 2
    freqs = 10000.0 ** (-jnp.arange(half_size, dtype=jnp.float32) / half_size)
    angles = positions.astype(jnp.float32)[:, None] * freqs[None, :]
    cosine = jnp.cos(angles)[:, None, None, :]
    sine = jnp.sin(angles)[:, None, None, :]
    first = vectors[..., :half_size]
    second = vectors[..., half_size:]
    return jnp.concatenate([first * cosine - second * sine, first * sine + second * cosine], axis=-1)

def layer_step(queue_state, modulation, sigma_step, block_position, w_query, w_key, w_value, w_output):
    head_count = HEAD_DEV * N_HEAD
    wide_rows = queue_state.astype(jnp.float32).reshape(BLOCKS, TOK_CH, D)
    row_mean = lax.optimization_barrier(jnp.mean(wide_rows, axis=-1, keepdims=True))
    row_var = lax.optimization_barrier(jnp.mean((wide_rows - row_mean) ** 2, axis=-1, keepdims=True))
    normed = (wide_rows - row_mean) * lax.rsqrt(row_var + 1e-06)
    modulated = (normed * (1.0 + modulation[:, 1][:, None, :]) + modulation[:, 0][:, None, :]).astype(jnp.bfloat16).reshape(TOKENS, D)
    shape4 = (BLOCKS, TOK_CH, head_count, HEAD_SIZE)
    queries = rotate(norm_heads(jnp.dot(modulated, w_query, preferred_element_type=jnp.float32).reshape(shape4)), block_position).astype(jnp.bfloat16)
    key_rows = rotate(norm_heads(jnp.dot(modulated, w_key, preferred_element_type=jnp.float32).reshape(shape4)), block_position).astype(jnp.bfloat16)
    values = jnp.dot(modulated, w_value, preferred_element_type=jnp.float32).astype(jnp.bfloat16).reshape(shape4)
    padding = ((REACH, REACH), (0, 0), (0, 0), (0, 0))
    key_padded = jnp.pad(key_rows, padding)
    value_padded = jnp.pad(values, padding)
    span_blocks = 2 * REACH + 1

    def one_block(block):
        keys_near = lax.dynamic_slice_in_dim(key_padded, block, span_blocks, 0).reshape(span_blocks * TOK_CH, head_count, HEAD_SIZE).astype(jnp.float32)
        values_near = lax.dynamic_slice_in_dim(value_padded, block, span_blocks, 0).reshape(span_blocks * TOK_CH, head_count, HEAD_SIZE).astype(jnp.float32)
        near_block = block - REACH + jnp.arange(span_blocks * TOK_CH, dtype=jnp.int32) // TOK_CH
        allowed = (near_block >= 0) & (near_block < BLOCKS)
        query_here = lax.dynamic_index_in_dim(queries, block, 0, keepdims=False).astype(jnp.float32)
        scores = jnp.einsum('qhd,khd->hqk', query_here, keys_near) / math.sqrt(HEAD_SIZE)
        raised = jnp.where(allowed[None, None, :], jnp.exp(scores), 0.0)
        weights = (raised / lax.optimization_barrier(jnp.sum(raised, axis=-1, keepdims=True))).astype(jnp.bfloat16)
        attended = jnp.einsum('hqk,khd->qhd', weights.astype(jnp.float32), values_near)
        return attended.astype(jnp.bfloat16).reshape(TOK_CH, head_count * HEAD_SIZE)
    attended = lax.map(one_block, jnp.arange(BLOCKS, dtype=jnp.int32)).reshape(TOKENS, head_count * HEAD_SIZE)
    group_width = HEAD_DEV * HEAD_SIZE
    mixed_out = jnp.zeros((TOKENS, D), jnp.float32)
    for group_index in range(N_HEAD):
        lower = group_index * group_width
        product = jnp.dot(attended[:, lower:lower + group_width], w_output[lower:lower + group_width], preferred_element_type=jnp.float32)
        rounded = lax.optimization_barrier(product.astype(jnp.bfloat16))
        mixed_out = mixed_out + rounded.astype(jnp.float32)
    layer_out = wide_rows + modulation[:, 2][:, None, :] * mixed_out.reshape(BLOCKS, TOK_CH, D)
    following = wide_rows + sigma_step[:, None, None] * layer_out
    return (layer_out.astype(jnp.bfloat16).reshape(TOKENS, D), following.astype(jnp.bfloat16).reshape(TOKENS, D))

def reference(queue, noise_block, w_query, w_key, w_value, w_output, mod_table, sigma_table, timestep_index, block_position):
    modulation = mod_table[timestep_index]
    sigma_step = sigma_table[timestep_index + 1] - sigma_table[timestep_index]
    first_out, first_state = layer_step(queue, modulation, sigma_step, block_position, w_query, w_key, w_value, w_output)
    shifted = jnp.concatenate([first_state[TOK_CH:], noise_block], axis=0)
    velocity, queue_out = layer_step(shifted, modulation, sigma_step, block_position, w_query, w_key, w_value, w_output)
    return (velocity, queue_out)
```

```python
import functools
import math

import jax
import jax.numpy as jnp
from jax import lax
from jax.experimental import pallas as pl
from jax.experimental.pallas import tpu as pltpu
from jax.sharding import PartitionSpec as P

HEAD_SIZE = 128
REACH = 2
MESH = pl.DeviceIdType.MESH
F32 = jnp.float32
BF16 = jnp.bfloat16


def kernel(
    F,
    H,
    queue_ref,
    noise_ref,
    wk_ref,
    wv_ref,
    wq_ref,
    wo_ref,
    mod_ref,
    sig_ref,
    cos_ref,
    sin_ref,
    vel_ref,
    out_ref,
    W,
    WO,
    ZA,
    ZB,
    MOD,
    NX,
    QB,
    KB,
    VB,
    ATT,
    own_sem,
    w_recv,
    w_up,
    w_dn,
    w_x,
    w_sib,
    o_yrecv,
    o_ysend,
    o_recv,
    o_up,
    o_dn,
    o_x,
    o_sib,
    q_recv,
    q_send,
    n_recv,
    n_send,
    a_recv,
    a_send,
    b_recv,
    b_send,
    k_recv,
    k_send,
    v_recv,
    v_send,
    t_recv,
    t_send,
):
    f = lax.axis_index("frame")
    h = lax.axis_index("head")
    Z = F // 4
    zs = Z // H
    z = f // 4
    x = (f // 2) % 2
    c = f % 2
    R, inner = wk_ref.shape
    T, slab = queue_ref.shape
    half = T // 2
    NC = 640
    chunks = slab // NC
    heads = inner // HEAD_SIZE
    pending = []

    def fid(zz, xx, cc):
        return (zz * 2 + xx) * 2 + cc

    def head_at(step):
        return (h + step) % H

    def send(src, dst, ssem, rsem, to_f, to_h, when=None):
        def make():
            return pltpu.make_async_remote_copy(
                src_ref=src,
                dst_ref=dst,
                send_sem=ssem,
                recv_sem=rsem,
                device_id=(to_f, to_h),
                device_id_type=MESH,
            )

        guarded(when, lambda: make().start())
        pending.append((when, lambda: make().wait_send()))

    def guarded(when, action):
        if when is None:
            action()
        else:
            pl.when(when)(action)

    def arrived(dst, rsem, when=None):
        guarded(
            when,
            lambda: pltpu.make_async_remote_copy(
                src_ref=dst,
                dst_ref=dst,
                send_sem=rsem,
                recv_sem=rsem,
                device_id=(fid(z, x, 1 - c), h),
                device_id_type=MESH,
            ).wait_recv(),
        )

    barrier = pltpu.get_barrier_semaphore()
    greet = [
        (z < Z - 1, f + 4, h),
        (z > 0, f - 4, h),
        (None, fid(z, 1 - x, c), h),
        (None, fid(z, x, 1 - c), h),
        (f < F - 1, f + 1, h),
        (f > 0, f - 1, h),
    ]
    for step in range(1, H):
        greet += [
            (None, f, head_at(step)),
            (f < F - 1, f + 1, head_at(step)),
            (f > 0, f - 1, head_at(step)),
        ]
    for when, to_f, to_h in greet:
        guarded(
            when,
            lambda to_f=to_f, to_h=to_h: pl.semaphore_signal(
                barrier, inc=1, device_id=(to_f, to_h), device_id_type=MESH
            ),
        )
    always = sum(when is None for when, _, _ in greet)
    sometimes = sum(when.astype(jnp.int32) for when, _, _ in greet if when is not None)
    pl.semaphore_wait(barrier, always + sometimes)

    shards = [wk_ref, wv_ref, wq_ref]

    def slot(m, zz, xx, cc):
        return W.at[m, pl.ds(pl.multiple_of(fid(zz, xx, cc) * R, 32), R), :]

    def spread_w(m, zz, src, up, down):
        dst = slot(m, zz, x, c)
        rsem = w_recv.at[m, fid(zz, x, c)]
        if up:
            send(src, dst, w_up.at[m, zz], rsem, f + 4, h, when=up[0])
        if down:
            send(src, dst, w_dn.at[m, zz], rsem, f - 4, h, when=down[0])
        send(src, dst, w_x.at[m, zz], rsem, fid(z, 1 - x, c), h, when=(up or down)[1])
        send(src, dst, w_sib.at[m, zz, x], rsem, fid(z, x, 1 - c), h, when=(up or down)[1])

    def w_own(m):
        spread_w(m, z, shards[m], (z < Z - 1, None), (z > 0, None))

    def w_along(m, d):
        below = z - d >= 0
        arrived(slot(m, z - d, x, c), w_recv.at[m, fid(z - d, x, c)], when=below)
        spread_w(m, z - d, slot(m, z - d, x, c), (below & (z < Z - 1), below), None)
        above = z + d <= Z - 1
        arrived(slot(m, z + d, x, c), w_recv.at[m, fid(z + d, x, c)], when=above)
        spread_w(m, z + d, slot(m, z + d, x, c), None, (above & (z > 0), above))

    def w_across(m, d):
        for zz, ok in ((z - d, z - d >= 0), (z + d, z + d <= Z - 1))[: 2 if d else 1]:
            ok = ok if d else None
            piece = slot(m, zz, 1 - x, c)
            rsem = w_recv.at[m, fid(zz, 1 - x, c)]
            arrived(piece, rsem, when=ok)
            send(piece, piece, w_sib.at[m, zz, 1 - x], rsem, fid(z, x, 1 - c), h, when=ok)

    def w_last(m):
        for zz in range(Z):
            for xx in range(2):
                arrived(slot(m, zz, xx, 1 - c), w_recv.at[m, fid(zz, xx, 1 - c)])
        pltpu.make_async_copy(shards[m], slot(m, z, x, c), own_sem.at[m]).wait()

    def o_slot(g, j, xx, cc):
        return WO.at[g, pl.ds(pl.multiple_of(fid(j, xx, cc) * R, 32), R), :]

    mine = z // zs
    here = mine == h
    rank = z - mine * zs

    def o_turn(i):
        j = jnp.where(z <= h * zs, i, zs - 1 - i)
        zz = h * zs + j
        for g in range(H):
            piece = o_slot(g, j, x, c)
            rsem = o_recv.at[g, fid(j, x, c)]
            arrived(piece, rsem, when=zz != z)
            arrived(piece, o_yrecv.at[g], when=(zz == z) & (h != g))
            send(piece, piece, o_up.at[g, j], rsem, f + 4, h, when=(zz <= z) & (z < Z - 1))
            send(piece, piece, o_dn.at[g, j], rsem, f - 4, h, when=(zz >= z) & (z > 0))
            send(piece, piece, o_x.at[g, j], rsem, fid(z, 1 - x, c), h)
            send(piece, piece, o_sib.at[g, j, x], rsem, fid(z, x, 1 - c), h)

    def o_across(i):
        j = jnp.where(z <= h * zs, i, zs - 1 - i)
        for g in range(H):
            piece = o_slot(g, j, 1 - x, c)
            rsem = o_recv.at[g, fid(j, 1 - x, c)]
            arrived(piece, rsem)
            send(piece, piece, o_sib.at[g, j, 1 - x], rsem, fid(z, x, 1 - c), h)

    def o_last():
        for g in range(H):
            for j in range(zs):
                for xx in range(2):
                    arrived(o_slot(g, j, xx, 1 - c), o_recv.at[g, fid(j, xx, 1 - c)])

    w_own(0)
    for step in range(1, H):
        send(queue_ref, ZA.at[h], q_send.at[step], q_recv.at[h], f, head_at(step))
    queue_own = pltpu.make_async_copy(queue_ref, ZA.at[h], own_sem.at[4])
    queue_own.start()
    for m in range(3):
        pltpu.make_async_copy(shards[m], slot(m, z, x, c), own_sem.at[m]).start()
    o_own = lambda: pltpu.make_async_copy(wo_ref, o_slot(h, rank, x, c), own_sem.at[3])
    guarded(here, lambda: o_own().start())
    guarded(here, lambda: o_own().wait())
    send(wo_ref, o_slot(h, rank, x, c), o_ysend.at[0], o_yrecv.at[h], f, mine, when=mine != h)
    last = f == F - 1
    noise_own = lambda: pltpu.make_async_copy(
        noise_ref, ZB.at[h, pl.ds(half, half), :], own_sem.at[5]
    )
    guarded(last, lambda: noise_own().start())
    for step in range(1, H):
        send(
            noise_ref,
            ZB.at[h, pl.ds(half, half), :],
            n_send.at[step],
            n_recv.at[h],
            f,
            head_at(step),
            when=last,
        )
    for s in range(2):

        @pl.when(f == 0)
        def _(s=s):
            KB[s, :T] = jnp.zeros((T, inner), BF16)
            VB[s, :T] = jnp.zeros((T, inner), BF16)

        @pl.when(last)
        def _(s=s):
            KB[s, 2 * T :] = jnp.zeros((T, inner), BF16)
            VB[s, 2 * T :] = jnp.zeros((T, inner), BF16)

    def modulate(src):
        rows = 16
        for b in range(2):

            def body(i, carry, b=b):
                at = pl.ds(pl.multiple_of(b * half + i * rows, rows), rows)
                wide = [src[g, at, :].astype(F32) for g in range(H)]
                total = sum(jnp.sum(w, axis=-1, keepdims=True) for w in wide)
                mean = total / (H * slab)
                wide = [w - mean for w in wide]
                square = sum(jnp.sum(w * w, axis=-1, keepdims=True) for w in wide)
                scale_by = lax.rsqrt(square / (H * slab) + 1e-06)
                for g in range(H):
                    shift = mod_ref[pl.ds((b * 3) * H + g, 1), :]
                    scale = mod_ref[pl.ds((b * 3 + 1) * H + g, 1), :]
                    MOD[g, at, :] = (wide[g] * scale_by * (1.0 + scale) + shift).astype(BF16)
                return carry

            lax.fori_loop(0, half // rows, body, 0)

    depth = 1280 if slab % 1280 == 0 else slab

    def project(m):
        total = jnp.zeros((T, inner), F32)
        for g in range(H):

            def body(i, acc, g=g):
                at = pl.multiple_of(i * depth, 128)
                return acc + jnp.dot(
                    MOD[g, :, pl.ds(at, depth)],
                    W[m, pl.ds(g * slab + at, depth), :],
                    preferred_element_type=F32,
                )

            total = lax.fori_loop(0, slab // depth, body, total)
        return total

    def rotated(full):
        parts = []
        for i in range(heads):
            one = full[:, i * HEAD_SIZE : (i + 1) * HEAD_SIZE]
            one = one * lax.rsqrt(jnp.mean(one * one, axis=-1, keepdims=True) + 1e-06)
            turned = pltpu.roll(one, HEAD_SIZE // 2, 1)
            parts.append((one * cos_ref[...] + turned * sin_ref[...]).astype(BF16))
        return parts

    def keys(s):
        for i, part in enumerate(rotated(project(0))):
            KB[s, T : 2 * T, i * HEAD_SIZE : (i + 1) * HEAD_SIZE] = part
        halo(KB, s, k_send, k_recv)

    def values(s):
        VB[s, T : 2 * T, :] = project(1).astype(BF16)
        halo(VB, s, v_send, v_recv)

    def halo(buf, s, ssem, rsem):
        mid = buf.at[s, pl.ds(T, T), :]
        send(mid, buf.at[s, pl.ds(0, T), :], ssem.at[s, 0], rsem.at[s, 0], f + 1, h, when=f < F - 1)
        send(mid, buf.at[s, pl.ds(2 * T, T), :], ssem.at[s, 1], rsem.at[s, 1], f - 1, h, when=f > 0)

    def queries(s):
        for i, part in enumerate(rotated(project(2))):
            QB[:, i * HEAD_SIZE : (i + 1) * HEAD_SIZE] = part

    def attend(s):
        for buf, rsem in ((KB, k_recv), (VB, v_recv)):
            arrived(buf.at[s, pl.ds(0, T), :], rsem.at[s, 0], when=f > 0)
            arrived(buf.at[s, pl.ds(2 * T, T), :], rsem.at[s, 1], when=f < F - 1)
        shape = (T, 3 * T)
        qb = lax.broadcasted_iota(jnp.int32, shape, 0) // half
        kb = lax.broadcasted_iota(jnp.int32, shape, 1) // half - 2
        near = (kb - qb <= REACH) & (qb - kb <= REACH)
        near = near & (kb + 2 * f >= 0) & (kb + 2 * f < 2 * F)
        for i in range(heads):
            cols = slice(i * HEAD_SIZE, (i + 1) * HEAD_SIZE)
            scores = lax.dot_general(
                QB[:, cols], KB[s, :, cols], (((1,), (1,)), ((), ())), preferred_element_type=F32
            )
            raised = jnp.where(near, jnp.exp(scores * (1.0 / math.sqrt(HEAD_SIZE))), 0.0)
            weights = raised / jnp.sum(raised, axis=-1, keepdims=True)
            ATT[s, h, :, cols] = jnp.dot(
                weights.astype(BF16), VB[s, :, cols], preferred_element_type=F32
            ).astype(BF16)
        for step in range(1, H):
            send(ATT.at[s, h], ATT.at[s, h], t_send.at[s, step], t_recv.at[s, h], f, head_at(step))

    def attended_all(s):
        for step in range(1, H):
            g = head_at(step)
            arrived(ATT.at[s, g], t_recv.at[s, g])

    def advance(s, src):
        for n in range(chunks):
            cols = slice(n * NC, (n + 1) * NC)
            mixed = None
            for g in range(H):
                product = lax.dot_general(
                    ATT[s, g],
                    WO[g, cols, :],
                    (((1,), (1,)), ((), ())),
                    preferred_element_type=F32,
                )
                product = product.astype(BF16).astype(F32)
                mixed = product if mixed is None else mixed + product
            for b in range(2):
                rows = slice(b * half, (b + 1) * half)
                base = src[h, rows, cols].astype(F32)
                gate = mod_ref[pl.ds((b * 3 + 2) * H + h, 1), cols]
                layer_out = base + gate * mixed[rows]
                following = (base + sig_ref[b : b + 1, 0:1] * layer_out).astype(BF16)
                if s == 1:
                    vel_ref[rows, cols] = layer_out.astype(BF16)
                    out_ref[rows, cols] = following
                elif b == 0:
                    NX[:, cols] = following
                else:
                    ZB[h, :half, cols] = following
            if s == 0:
                at = pl.ds(n * NC, NC)
                low = ZB.at[h, pl.ds(0, half), at]
                high = ZB.at[h, pl.ds(half, half), at]
                for step in range(H):
                    to_h = head_at(step)
                    if step:
                        send(low, low, a_send.at[step, n], a_recv.at[h, n], f, to_h)
                    send(
                        NX.at[:, at],
                        high,
                        b_send.at[step, n],
                        b_recv.at[h, n],
                        f - 1,
                        to_h,
                        when=f > 0,
                    )

    def second_state():
        for step in range(H):
            g = head_at(step)
            for n in range(chunks):
                at = pl.ds(n * NC, NC)
                if step:
                    arrived(ZB.at[g, pl.ds(0, half), at], a_recv.at[g, n])
                arrived(ZB.at[g, pl.ds(half, half), at], b_recv.at[g, n], when=f < F - 1)
            if step:
                arrived(ZB.at[g, pl.ds(half, half), :], n_recv.at[g], when=last)
        guarded(last, lambda: noise_own().wait())

    w_along(0, 1)
    w_own(1)
    w_across(0, 0)
    for d in range(2, Z):
        w_along(0, d)
        w_across(0, d - 1)
    w_along(1, 1)
    for step in range(1, H):
        g = head_at(step)
        arrived(ZA.at[g], q_recv.at[g])
    queue_own.wait()
    modulate(ZA)
    w_across(0, Z - 1)
    w_own(2)
    w_last(0)
    w_across(1, 0)
    keys(0)
    for d in range(2, Z):
        w_along(1, d)
        w_across(1, d - 1)
    w_along(2, 1)
    w_across(1, Z - 1)
    w_last(1)
    w_across(2, 0)
    values(0)
    for d in range(2, Z):
        w_along(2, d)
        w_across(2, d - 1)
    o_turn(0)
    w_across(2, Z - 1)
    w_last(2)
    queries(0)
    o_across(0)
    for i in range(1, zs):
        o_turn(i)
    attend(0)
    for i in range(1, zs):
        o_across(i)
    o_last()
    attended_all(0)
    advance(0, ZA)
    second_state()
    modulate(ZB)
    keys(1)
    values(1)
    queries(1)
    attend(1)
    attended_all(1)
    advance(1, ZB)
    for when, action in pending:
        guarded(when, action)


def per_device(
    queue,
    noise_block,
    w_query,
    w_key,
    w_value,
    w_output,
    mod_table,
    sigma_table,
    timestep_index,
    block_position,
):
    F = lax.axis_size("frame")
    H = lax.axis_size("head")
    T, slab = queue.shape
    blocks = timestep_index.shape[0]
    half = T // blocks
    R, inner = w_key.shape
    Z = F // 4
    zs = Z // H
    chunks = slab // 640
    modulation = jnp.concatenate(
        [lax.dynamic_slice_in_dim(mod_table, timestep_index[b], 1, 0) for b in range(blocks)]
    ).reshape(blocks * 3 * H, slab)
    sigma_step = jnp.stack(
        [
            lax.dynamic_index_in_dim(sigma_table, timestep_index[b] + 1, 0, False)
            - lax.dynamic_index_in_dim(sigma_table, timestep_index[b], 0, False)
            for b in range(blocks)
        ]
    )
    sigma_rows = jnp.broadcast_to(sigma_step[:, None], (blocks, 128))
    half_size = HEAD_SIZE // 2
    freqs = 10000.0 ** (-jnp.arange(half_size, dtype=F32) / half_size)
    angles = block_position.astype(F32)[:, None] * freqs[None, :]
    cosine, sine = jnp.cos(angles), jnp.sin(angles)
    cosine = jnp.repeat(jnp.concatenate([cosine, cosine], axis=-1), half, axis=0)
    sine = jnp.repeat(jnp.concatenate([-sine, sine], axis=-1), half, axis=0)
    dma = pltpu.SemaphoreType.DMA
    vmem = pl.BlockSpec(memory_space=pltpu.VMEM)
    hbm = pl.BlockSpec(memory_space=pl.ANY)
    out = jax.ShapeDtypeStruct((T, slab), BF16)
    return pl.pallas_call(
        functools.partial(kernel, F, H),
        out_shape=(out, out),
        in_specs=[hbm] * 6 + [vmem] * 4,
        out_specs=(vmem, vmem),
        scratch_shapes=[
            pltpu.VMEM((3, F * R, inner), BF16),
            pltpu.VMEM((H, 4 * zs * R, inner), BF16),
            pltpu.VMEM((H, T, slab), BF16),
            pltpu.VMEM((H, T, slab), BF16),
            pltpu.VMEM((H, T, slab), BF16),
            pltpu.VMEM((half, slab), BF16),
            pltpu.VMEM((T, inner), BF16),
            pltpu.VMEM((2, 3 * T, inner), BF16),
            pltpu.VMEM((2, 3 * T, inner), BF16),
            pltpu.VMEM((2, H, T, inner), BF16),
            dma((6,)),
            dma((3, F)),
            dma((3, Z)),
            dma((3, Z)),
            dma((3, Z)),
            dma((3, Z, 2)),
            dma((H,)),
            dma((1,)),
            dma((H, 4 * zs)),
            dma((H, zs)),
            dma((H, zs)),
            dma((H, zs)),
            dma((H, zs, 2)),
            dma((H,)),
            dma((H,)),
            dma((H,)),
            dma((H,)),
            dma((H, chunks)),
            dma((H, chunks)),
            dma((H, chunks)),
            dma((H, chunks)),
            dma((2, 2)),
            dma((2, 2)),
            dma((2, 2)),
            dma((2, 2)),
            dma((2, H)),
            dma((2, H)),
        ],
        compiler_params=pltpu.CompilerParams(
            collective_id=0, has_side_effects=True, vmem_limit_bytes=48 * 1024 * 1024
        ),
        cost_estimate=pl.CostEstimate(
            flops=4 * T * H * slab * inner * 4, bytes_accessed=8 * R * inner * 2, transcendentals=0
        ),
    )(
        queue,
        noise_block,
        w_key,
        w_value,
        w_query,
        w_output.T,
        modulation,
        sigma_rows,
        cosine,
        sine,
    )


def solution(mesh):
    in_specs = (
        P("frame", "head"),
        P(None, "head"),
        P("frame", "head"),
        P("frame", "head"),
        P("frame", "head"),
        P("head", "frame"),
        P(),
        P(),
        P("frame"),
        P("frame"),
    )
    out_specs = (P("frame", "head"), P("frame", "head"))
    return jax.shard_map(
        per_device, mesh=mesh, in_specs=in_specs, out_specs=out_specs, check_vma=False
    )
```

```python
import functools
import math

import jax
import jax.numpy as jnp
import numpy as np
from jax import lax
from jax.experimental import pallas as pl
from jax.experimental.pallas import tpu as pltpu
from jax.sharding import PartitionSpec as P

HEAD_SIZE = 128
REACH = 2
MESH = pl.DeviceIdType.MESH
F32 = jnp.float32
BF16 = jnp.bfloat16


def kernel(
    F,
    H,
    queue_ref,
    noise_ref,
    wk_ref,
    wv_ref,
    wq_ref,
    wo_ref,
    table_ref,
    freq_ref,
    sigma_ref,
    level_ref,
    pos_ref,
    vel_ref,
    out_ref,
    W,
    WO,
    ZA,
    ZB,
    MOD,
    NX,
    QB,
    KB,
    VB,
    ATT,
    table,
    mod_ref,
    cos_ref,
    sin_ref,
    own_sem,
    w_recv,
    w_up,
    w_dn,
    w_x,
    w_sib,
    o_yrecv,
    o_ysend,
    o_recv,
    o_up,
    o_dn,
    o_x,
    o_sib,
    q_recv,
    q_send,
    n_recv,
    n_send,
    a_recv,
    a_send,
    b_recv,
    b_send,
    k_recv,
    k_send,
    v_recv,
    v_send,
    t_recv,
    t_send,
):
    f = lax.axis_index("frame")
    h = lax.axis_index("head")
    Z = F // 4
    zs = Z // H
    z = f // 4
    x = (f // 2) % 2
    c = f % 2
    R, inner = wk_ref.shape
    T, slab = queue_ref.shape
    half = T // 2
    NC = 640
    chunks = slab // NC
    heads = inner // HEAD_SIZE
    pending = []

    def fid(zz, xx, cc):
        return (zz * 2 + xx) * 2 + cc

    def head_at(step):
        return (h + step) % H

    def send(src, dst, ssem, rsem, to_f, to_h, when=None):
        def make():
            return pltpu.make_async_remote_copy(
                src_ref=src,
                dst_ref=dst,
                send_sem=ssem,
                recv_sem=rsem,
                device_id=(to_f, to_h),
                device_id_type=MESH,
            )

        guarded(when, lambda: make().start())
        pending.append((when, lambda: make().wait_send()))

    def guarded(when, action):
        if when is None:
            action()
        else:
            pl.when(when)(action)

    def arrived(dst, rsem, when=None):
        guarded(
            when,
            lambda: pltpu.make_async_remote_copy(
                src_ref=dst,
                dst_ref=dst,
                send_sem=rsem,
                recv_sem=rsem,
                device_id=(fid(z, x, 1 - c), h),
                device_id_type=MESH,
            ).wait_recv(),
        )

    barrier = pltpu.get_barrier_semaphore()
    greet = [
        (z < Z - 1, f + 4, h),
        (z > 0, f - 4, h),
        (None, fid(z, 1 - x, c), h),
        (None, fid(z, x, 1 - c), h),
        (f < F - 1, f + 1, h),
        (f > 0, f - 1, h),
    ]
    for step in range(1, H):
        greet += [
            (None, f, head_at(step)),
            (f < F - 1, f + 1, head_at(step)),
            (f > 0, f - 1, head_at(step)),
        ]
    for when, to_f, to_h in greet:
        guarded(
            when,
            lambda to_f=to_f, to_h=to_h: pl.semaphore_signal(
                barrier, inc=1, device_id=(to_f, to_h), device_id_type=MESH
            ),
        )
    always = sum(when is None for when, _, _ in greet)
    sometimes = sum(when.astype(jnp.int32) for when, _, _ in greet if when is not None)
    pl.semaphore_wait(barrier, always + sometimes)

    shards = [wk_ref, wv_ref, wq_ref]

    def slot(m, zz, xx, cc):
        return W.at[m, pl.ds(pl.multiple_of(fid(zz, xx, cc) * R, 32), R), :]

    def spread_w(m, zz, src, up, down):
        dst = slot(m, zz, x, c)
        rsem = w_recv.at[m, fid(zz, x, c)]
        if up:
            send(src, dst, w_up.at[m, zz], rsem, f + 4, h, when=up[0])
        if down:
            send(src, dst, w_dn.at[m, zz], rsem, f - 4, h, when=down[0])
        send(src, dst, w_x.at[m, zz], rsem, fid(z, 1 - x, c), h, when=(up or down)[1])
        send(src, dst, w_sib.at[m, zz, x], rsem, fid(z, x, 1 - c), h, when=(up or down)[1])

    def w_own(m):
        spread_w(m, z, shards[m], (z < Z - 1, None), (z > 0, None))

    def w_along(m, d):
        below = z - d >= 0
        arrived(slot(m, z - d, x, c), w_recv.at[m, fid(z - d, x, c)], when=below)
        spread_w(m, z - d, slot(m, z - d, x, c), (below & (z < Z - 1), below), None)
        above = z + d <= Z - 1
        arrived(slot(m, z + d, x, c), w_recv.at[m, fid(z + d, x, c)], when=above)
        spread_w(m, z + d, slot(m, z + d, x, c), None, (above & (z > 0), above))

    def w_across(m, d):
        for zz, ok in ((z - d, z - d >= 0), (z + d, z + d <= Z - 1))[: 2 if d else 1]:
            ok = ok if d else None
            piece = slot(m, zz, 1 - x, c)
            rsem = w_recv.at[m, fid(zz, 1 - x, c)]
            arrived(piece, rsem, when=ok)
            send(piece, piece, w_sib.at[m, zz, 1 - x], rsem, fid(z, x, 1 - c), h, when=ok)

    def w_last(m):
        for zz in range(Z):
            for xx in range(2):
                arrived(slot(m, zz, xx, 1 - c), w_recv.at[m, fid(zz, xx, 1 - c)])
        pltpu.make_async_copy(shards[m], slot(m, z, x, c), own_sem.at[m]).wait()

    def o_slot(g, j, xx, cc):
        return WO.at[g, pl.ds(pl.multiple_of(fid(j, xx, cc) * R, 32), R), :]

    mine = z // zs
    here = mine == h
    rank = z - mine * zs

    def o_turn(i):
        j = jnp.where(z <= h * zs, i, zs - 1 - i)
        zz = h * zs + j
        for g in range(H):
            piece = o_slot(g, j, x, c)
            rsem = o_recv.at[g, fid(j, x, c)]
            arrived(piece, rsem, when=zz != z)
            arrived(piece, o_yrecv.at[g], when=(zz == z) & (h != g))
            send(piece, piece, o_up.at[g, j], rsem, f + 4, h, when=(zz <= z) & (z < Z - 1))
            send(piece, piece, o_dn.at[g, j], rsem, f - 4, h, when=(zz >= z) & (z > 0))
            send(piece, piece, o_x.at[g, j], rsem, fid(z, 1 - x, c), h)
            send(piece, piece, o_sib.at[g, j, x], rsem, fid(z, x, 1 - c), h)

    def o_across(i):
        j = jnp.where(z <= h * zs, i, zs - 1 - i)
        for g in range(H):
            piece = o_slot(g, j, 1 - x, c)
            rsem = o_recv.at[g, fid(j, 1 - x, c)]
            arrived(piece, rsem)
            send(piece, piece, o_sib.at[g, j, 1 - x], rsem, fid(z, x, 1 - c), h)

    def o_last():
        for g in range(H):
            for j in range(zs):
                for xx in range(2):
                    arrived(o_slot(g, j, xx, 1 - c), o_recv.at[g, fid(j, xx, 1 - c)])

    w_own(0)
    table_own = pltpu.make_async_copy(table_ref, table, own_sem.at[6])
    table_own.start()
    for step in range(1, H):
        send(queue_ref, ZA.at[h], q_send.at[step], q_recv.at[h], f, head_at(step))
    queue_own = pltpu.make_async_copy(queue_ref, ZA.at[h], own_sem.at[4])
    queue_own.start()
    for m in range(3):
        pltpu.make_async_copy(shards[m], slot(m, z, x, c), own_sem.at[m]).start()
    o_own = lambda: pltpu.make_async_copy(wo_ref, o_slot(h, rank, x, c), own_sem.at[3])
    guarded(here, lambda: o_own().start())
    guarded(here, lambda: o_own().wait())
    send(wo_ref, o_slot(h, rank, x, c), o_ysend.at[0], o_yrecv.at[h], f, mine, when=mine != h)
    last = f == F - 1
    noise_own = lambda: pltpu.make_async_copy(
        noise_ref, ZB.at[h, pl.ds(half, half), :], own_sem.at[5]
    )
    guarded(last, lambda: noise_own().start())
    for step in range(1, H):
        send(
            noise_ref,
            ZB.at[h, pl.ds(half, half), :],
            n_send.at[step],
            n_recv.at[h],
            f,
            head_at(step),
            when=last,
        )
    for s in range(2):

        @pl.when(f == 0)
        def _(s=s):
            KB[s, :T] = jnp.zeros((T, inner), BF16)
            VB[s, :T] = jnp.zeros((T, inner), BF16)

        @pl.when(last)
        def _(s=s):
            KB[s, 2 * T :] = jnp.zeros((T, inner), BF16)
            VB[s, 2 * T :] = jnp.zeros((T, inner), BF16)

    def tables():
        lane = lax.broadcasted_iota(jnp.int32, (1, HEAD_SIZE), 1)
        sign = jnp.where(lane < HEAD_SIZE // 2, -1.0, 1.0)
        for b in range(2):
            level = level_ref[b]
            for k in range(3):
                for g in range(H):
                    mod_ref[(b * 3 + k) * H + g : (b * 3 + k) * H + g + 1, :] = table[
                        k, pl.ds(level, 1), g * slab : (g + 1) * slab
                    ]
            angles = freq_ref[...] * pos_ref[b].astype(F32)
            rows = slice(b * half, (b + 1) * half)
            cos_ref[rows, :] = jnp.broadcast_to(jnp.cos(angles), (half, HEAD_SIZE))
            sin_ref[rows, :] = jnp.broadcast_to(jnp.sin(angles) * sign, (half, HEAD_SIZE))

    def sigma_step(b):
        return sigma_ref[level_ref[b] + 1] - sigma_ref[level_ref[b]]

    def modulate(src):
        rows = 16
        for b in range(2):

            def body(i, carry, b=b):
                at = pl.ds(pl.multiple_of(b * half + i * rows, rows), rows)
                wide = [src[g, at, :].astype(F32) for g in range(H)]
                total = sum(jnp.sum(w, axis=-1, keepdims=True) for w in wide)
                mean = total / (H * slab)
                wide = [w - mean for w in wide]
                square = sum(jnp.sum(w * w, axis=-1, keepdims=True) for w in wide)
                scale_by = lax.rsqrt(square / (H * slab) + 1e-06)
                for g in range(H):
                    shift = mod_ref[pl.ds((b * 3) * H + g, 1), :]
                    scale = mod_ref[pl.ds((b * 3 + 1) * H + g, 1), :]
                    MOD[g, at, :] = (wide[g] * scale_by * (1.0 + scale) + shift).astype(BF16)
                return carry

            lax.fori_loop(0, half // rows, body, 0)

    depth = 1280 if slab % 1280 == 0 else slab

    def project(m):
        total = jnp.zeros((T, inner), F32)
        for g in range(H):

            def body(i, acc, g=g):
                at = pl.multiple_of(i * depth, 128)
                return acc + jnp.dot(
                    MOD[g, :, pl.ds(at, depth)],
                    W[m, pl.ds(g * slab + at, depth), :],
                    preferred_element_type=F32,
                )

            total = lax.fori_loop(0, slab // depth, body, total)
        return total

    def rotated(full):
        parts = []
        for i in range(heads):
            one = full[:, i * HEAD_SIZE : (i + 1) * HEAD_SIZE]
            one = one * lax.rsqrt(jnp.mean(one * one, axis=-1, keepdims=True) + 1e-06)
            turned = pltpu.roll(one, HEAD_SIZE // 2, 1)
            parts.append((one * cos_ref[...] + turned * sin_ref[...]).astype(BF16))
        return parts

    def keys(s):
        for i, part in enumerate(rotated(project(0))):
            KB[s, T : 2 * T, i * HEAD_SIZE : (i + 1) * HEAD_SIZE] = part
        halo(KB, s, k_send, k_recv)

    def values(s):
        VB[s, T : 2 * T, :] = project(1).astype(BF16)
        halo(VB, s, v_send, v_recv)

    def halo(buf, s, ssem, rsem):
        mid = buf.at[s, pl.ds(T, T), :]
        send(mid, buf.at[s, pl.ds(0, T), :], ssem.at[s, 0], rsem.at[s, 0], f + 1, h, when=f < F - 1)
        send(mid, buf.at[s, pl.ds(2 * T, T), :], ssem.at[s, 1], rsem.at[s, 1], f - 1, h, when=f > 0)

    def queries(s):
        for i, part in enumerate(rotated(project(2))):
            QB[:, i * HEAD_SIZE : (i + 1) * HEAD_SIZE] = part

    def attend(s):
        for buf, rsem in ((KB, k_recv), (VB, v_recv)):
            arrived(buf.at[s, pl.ds(0, T), :], rsem.at[s, 0], when=f > 0)
            arrived(buf.at[s, pl.ds(2 * T, T), :], rsem.at[s, 1], when=f < F - 1)
        shape = (T, 3 * T)
        qb = lax.broadcasted_iota(jnp.int32, shape, 0) // half
        kb = lax.broadcasted_iota(jnp.int32, shape, 1) // half - 2
        near = (kb - qb <= REACH) & (qb - kb <= REACH)
        near = near & (kb + 2 * f >= 0) & (kb + 2 * f < 2 * F)
        for i in range(heads):
            cols = slice(i * HEAD_SIZE, (i + 1) * HEAD_SIZE)
            scores = lax.dot_general(
                QB[:, cols], KB[s, :, cols], (((1,), (1,)), ((), ())), preferred_element_type=F32
            )
            raised = jnp.where(near, jnp.exp(scores * (1.0 / math.sqrt(HEAD_SIZE))), 0.0)
            weights = raised / jnp.sum(raised, axis=-1, keepdims=True)
            ATT[s, h, :, cols] = jnp.dot(
                weights.astype(BF16), VB[s, :, cols], preferred_element_type=F32
            ).astype(BF16)
        for step in range(1, H):
            send(ATT.at[s, h], ATT.at[s, h], t_send.at[s, step], t_recv.at[s, h], f, head_at(step))

    def attended_all(s):
        for step in range(1, H):
            g = head_at(step)
            arrived(ATT.at[s, g], t_recv.at[s, g])

    def advance(s, src):
        for n in range(chunks):
            cols = slice(n * NC, (n + 1) * NC)
            mixed = None
            for g in range(H):
                product = lax.dot_general(
                    ATT[s, g],
                    WO[g, cols, :],
                    (((1,), (1,)), ((), ())),
                    preferred_element_type=F32,
                )
                product = product.astype(BF16).astype(F32)
                mixed = product if mixed is None else mixed + product
            for b in range(2):
                rows = slice(b * half, (b + 1) * half)
                base = src[h, rows, cols].astype(F32)
                gate = mod_ref[pl.ds((b * 3 + 2) * H + h, 1), cols]
                layer_out = base + gate * mixed[rows]
                following = (base + sigma_step(b) * layer_out).astype(BF16)
                if s == 1:
                    vel_ref[rows, cols] = layer_out.astype(BF16)
                    out_ref[rows, cols] = following
                elif b == 0:
                    NX[:, cols] = following
                else:
                    ZB[h, :half, cols] = following
            if s == 0:
                at = pl.ds(n * NC, NC)
                low = ZB.at[h, pl.ds(0, half), at]
                high = ZB.at[h, pl.ds(half, half), at]
                for step in range(H):
                    to_h = head_at(step)
                    if step:
                        send(low, low, a_send.at[step, n], a_recv.at[h, n], f, to_h)
                    send(
                        NX.at[:, at],
                        high,
                        b_send.at[step, n],
                        b_recv.at[h, n],
                        f - 1,
                        to_h,
                        when=f > 0,
                    )

    def second_state():
        for step in range(H):
            g = head_at(step)
            for n in range(chunks):
                at = pl.ds(n * NC, NC)
                if step:
                    arrived(ZB.at[g, pl.ds(0, half), at], a_recv.at[g, n])
                arrived(ZB.at[g, pl.ds(half, half), at], b_recv.at[g, n], when=f < F - 1)
            if step:
                arrived(ZB.at[g, pl.ds(half, half), :], n_recv.at[g], when=last)
        guarded(last, lambda: noise_own().wait())

    w_along(0, 1)
    w_own(1)
    w_across(0, 0)
    for d in range(2, Z):
        w_along(0, d)
        w_across(0, d - 1)
    w_along(1, 1)
    for step in range(1, H):
        g = head_at(step)
        arrived(ZA.at[g], q_recv.at[g])
    queue_own.wait()
    table_own.wait()
    tables()
    modulate(ZA)
    w_across(0, Z - 1)
    w_own(2)
    w_last(0)
    w_across(1, 0)
    keys(0)
    for d in range(2, Z):
        w_along(1, d)
        w_across(1, d - 1)
    w_along(2, 1)
    w_across(1, Z - 1)
    w_last(1)
    w_across(2, 0)
    values(0)
    for d in range(2, Z):
        w_along(2, d)
        w_across(2, d - 1)
    o_turn(0)
    w_across(2, Z - 1)
    w_last(2)
    queries(0)
    o_across(0)
    for i in range(1, zs):
        o_turn(i)
    attend(0)
    for i in range(1, zs):
        o_across(i)
    o_last()
    attended_all(0)
    advance(0, ZA)
    second_state()
    modulate(ZB)
    keys(1)
    values(1)
    queries(1)
    attend(1)
    attended_all(1)
    advance(1, ZB)
    for when, action in pending:
        guarded(when, action)


def per_device(
    queue,
    noise_block,
    w_query,
    w_key,
    w_value,
    w_output,
    mod_table,
    sigma_table,
    timestep_index,
    block_position,
):
    F = lax.axis_size("frame")
    H = lax.axis_size("head")
    T, slab = queue.shape
    blocks = timestep_index.shape[0]
    half = T // blocks
    levels = mod_table.shape[0]
    R, inner = w_key.shape
    Z = F // 4
    zs = Z // H
    chunks = slab // 640
    freqs = 10000.0 ** (-np.arange(HEAD_SIZE // 2) / (HEAD_SIZE // 2))
    freqs = jnp.asarray(np.concatenate([freqs, freqs])[None, :].astype(np.float32))
    dma = pltpu.SemaphoreType.DMA
    vmem = pl.BlockSpec(memory_space=pltpu.VMEM)
    smem = pl.BlockSpec(memory_space=pltpu.SMEM)
    hbm = pl.BlockSpec(memory_space=pl.ANY)
    out = jax.ShapeDtypeStruct((T, slab), BF16)
    return pl.pallas_call(
        functools.partial(kernel, F, H),
        out_shape=(out, out),
        in_specs=[hbm] * 7 + [vmem] + [smem] * 3,
        out_specs=(vmem, vmem),
        scratch_shapes=[
            pltpu.VMEM((3, F * R, inner), BF16),
            pltpu.VMEM((H, 4 * zs * R, inner), BF16),
            pltpu.VMEM((H, T, slab), BF16),
            pltpu.VMEM((H, T, slab), BF16),
            pltpu.VMEM((H, T, slab), BF16),
            pltpu.VMEM((half, slab), BF16),
            pltpu.VMEM((T, inner), BF16),
            pltpu.VMEM((2, 3 * T, inner), BF16),
            pltpu.VMEM((2, 3 * T, inner), BF16),
            pltpu.VMEM((2, H, T, inner), BF16),
            pltpu.VMEM((3, levels, H * slab), F32),
            pltpu.VMEM((blocks * 3 * H, slab), F32),
            pltpu.VMEM((T, HEAD_SIZE), F32),
            pltpu.VMEM((T, HEAD_SIZE), F32),
            dma((7,)),
            dma((3, F)),
            dma((3, Z)),
            dma((3, Z)),
            dma((3, Z)),
            dma((3, Z, 2)),
            dma((H,)),
            dma((1,)),
            dma((H, 4 * zs)),
            dma((H, zs)),
            dma((H, zs)),
            dma((H, zs)),
            dma((H, zs, 2)),
            dma((H,)),
            dma((H,)),
            dma((H,)),
            dma((H,)),
            dma((H, chunks)),
            dma((H, chunks)),
            dma((H, chunks)),
            dma((H, chunks)),
            dma((2, 2)),
            dma((2, 2)),
            dma((2, 2)),
            dma((2, 2)),
            dma((2, H)),
            dma((2, H)),
        ],
        compiler_params=pltpu.CompilerParams(
            collective_id=0, has_side_effects=True, vmem_limit_bytes=62 * 1024 * 1024
        ),
        cost_estimate=pl.CostEstimate(
            flops=4 * T * H * slab * inner * 4, bytes_accessed=8 * R * inner * 2, transcendentals=0
        ),
    )(
        queue,
        noise_block,
        w_key,
        w_value,
        w_query,
        w_output.T,
        jnp.transpose(mod_table, (1, 0, 2)),
        freqs,
        sigma_table,
        timestep_index,
        block_position,
    )


def solution(mesh):
    in_specs = (
        P("frame", "head"),
        P(None, "head"),
        P("frame", "head"),
        P("frame", "head"),
        P("frame", "head"),
        P("head", "frame"),
        P(),
        P(),
        P("frame"),
        P("frame"),
    )
    out_specs = (P("frame", "head"), P("frame", "head"))
    return jax.shard_map(
        per_device, mesh=mesh, in_specs=in_specs, out_specs=out_specs, check_vma=False
    )
```

```python
import functools
import math

import jax
import jax.numpy as jnp
import numpy as np
from jax import lax
from jax.experimental import pallas as pl
from jax.experimental.pallas import tpu as pltpu
from jax.sharding import PartitionSpec as P

HEAD_SIZE = 128
REACH = 2
MESH = pl.DeviceIdType.MESH
F32 = jnp.float32
BF16 = jnp.bfloat16


def kernel(
    F,
    H,
    queue_ref,
    noise_ref,
    wk_ref,
    wv_ref,
    wq_ref,
    wo_ref,
    table_ref,
    freq_ref,
    sigma_ref,
    level_ref,
    pos_ref,
    vel_ref,
    out_ref,
    W,
    ZL,
    ZA,
    ZB,
    MOD,
    NX,
    QB,
    KB,
    VB,
    ATT,
    PO,
    PS,
    PR,
    ST,
    table,
    mod_ref,
    cos_ref,
    sin_ref,
    own_sem,
    z_recv,
    z_up,
    z_dn,
    y_send,
    y_recv,
    x_send,
    x_recv,
    s_send,
    s_recv,
    l_sem,
    b_recv,
    b_send,
    k_recv,
    k_send,
    v_recv,
    v_send,
    t_recv,
    t_send,
    p_recv,
    p_send,
    st_recv,
    st_send,
):
    f = lax.axis_index("frame")
    h = lax.axis_index("head")
    Z = F // 4
    zs = Z // H
    z = f // 4
    x = (f // 2) % 2
    c = f % 2
    R, inner = wk_ref.shape
    T, slab = queue_ref.shape
    half = T // 2
    NC = 640
    chunks = slab // NC
    heads = inner // HEAD_SIZE
    pending = []

    def fid(zz, xx, cc):
        return (zz * 2 + xx) * 2 + cc

    def head_at(step):
        return (h + step) % H

    def send(src, dst, ssem, rsem, to_f, to_h, when=None):
        def make():
            return pltpu.make_async_remote_copy(
                src_ref=src,
                dst_ref=dst,
                send_sem=ssem,
                recv_sem=rsem,
                device_id=(to_f, to_h),
                device_id_type=MESH,
            )

        guarded(when, lambda: make().start())
        pending.append((when, lambda: make().wait_send()))

    def guarded(when, action):
        if when is None:
            action()
        else:
            pl.when(when)(action)

    def arrived(dst, rsem, when=None):
        guarded(
            when,
            lambda: pltpu.make_async_remote_copy(
                src_ref=dst,
                dst_ref=dst,
                send_sem=rsem,
                recv_sem=rsem,
                device_id=(fid(z, x, 1 - c), h),
                device_id_type=MESH,
            ).wait_recv(),
        )

    barrier = pltpu.get_barrier_semaphore()
    greet = [
        (z < Z - 1, f + 4, h),
        (z > 0, f - 4, h),
        (None, fid(z, 1 - x, c), h),
        (None, fid(z, x, 1 - c), h),
        (f < F - 1, f + 1, h),
        (f > 0, f - 1, h),
    ]
    for step in range(1, H):
        greet.append((None, f, head_at(step)))
    for when, to_f, to_h in greet:
        guarded(
            when,
            lambda to_f=to_f, to_h=to_h: pl.semaphore_signal(
                barrier, inc=1, device_id=(to_f, to_h), device_id_type=MESH
            ),
        )
    always = sum(when is None for when, _, _ in greet)
    sometimes = sum(when.astype(jnp.int32) for when, _, _ in greet if when is not None)
    pl.semaphore_wait(barrier, always + sometimes)

    shards = [wk_ref, wv_ref, wq_ref, wo_ref]

    def slot(m, g, j, xx, cc):
        return W.at[m, g, pl.ds(pl.multiple_of(fid(j, xx, cc) * R, 32), R), :]

    def both(one, other):
        return other if one is None else one & other

    def local(m, zz, src):
        j = zz - zz // zs * zs
        return pltpu.make_async_copy(src, slot(m, h, j, x, c), l_sem.at[m, j])

    def pass_on(m, g, j, src, when=None):
        dst = slot(m, g, j, x, c)
        send(src, dst, x_send.at[m, g, j], x_recv.at[m, g, j], fid(z, 1 - x, c), h, when=when)
        send(
            src, dst, s_send.at[m, g, j, x], s_recv.at[m, g, j, x], fid(z, x, 1 - c), h, when=when
        )

    def hand_out(m, zz, src, when=None):
        home = zz // zs
        j = zz - home * zs
        used = both(when, home == h)
        guarded(used, lambda: local(m, zz, src).start())
        pass_on(m, h, j, src, when=used)
        send(
            src,
            slot(m, h, j, x, c),
            y_send.at[m, zz],
            y_recv.at[m, h, j],
            f,
            home,
            when=both(when, home != h),
        )

    def w_own(m):
        src = shards[m]
        send(src, ZL.at[m, z], z_up.at[m, z], z_recv.at[m, z], f + 4, h, when=z < Z - 1)
        send(src, ZL.at[m, z], z_dn.at[m, z], z_recv.at[m, z], f - 4, h, when=z > 0)
        hand_out(m, z, src)

    def w_along(m, d):
        below, above = z - d >= 0, z + d <= Z - 1
        for zz, ok, up in ((z - d, below, True), (z + d, above, False)):
            piece = ZL.at[m, zz]
            arrived(piece, z_recv.at[m, zz], when=ok)
            if up:
                send(piece, piece, z_up.at[m, zz], z_recv.at[m, zz], f + 4, h, when=ok & (z < Z - 1))
            else:
                send(piece, piece, z_dn.at[m, zz], z_recv.at[m, zz], f - 4, h, when=ok & (z > 0))
            hand_out(m, zz, piece, when=ok)

    def turns():
        for i in range(zs):
            yield jnp.where(z <= h * zs, i, zs - 1 - i)

    def w_heads(m):
        for j in turns():
            for step in range(1, H):
                g = head_at(step)
                piece = slot(m, g, j, x, c)
                arrived(piece, y_recv.at[m, g, j])
                pass_on(m, g, j, piece)

    def w_across(m):
        for j in turns():
            for step in range(H):
                g = head_at(step)
                piece = slot(m, g, j, 1 - x, c)
                arrived(piece, x_recv.at[m, g, j])
                send(
                    piece,
                    piece,
                    s_send.at[m, g, j, 1 - x],
                    s_recv.at[m, g, j, 1 - x],
                    fid(z, x, 1 - c),
                    h,
                )

    def w_last(m):
        for j in range(zs):
            for g in range(H):
                for xx in range(2):
                    arrived(slot(m, g, j, xx, 1 - c), s_recv.at[m, g, j, xx])
            local(m, h * zs + j, shards[m]).wait()

    w_own(0)
    table_own = pltpu.make_async_copy(
        table_ref.at[:, :, pl.ds(pl.multiple_of(h * slab, 128), slab)], table, own_sem.at[0]
    )
    table_own.start()
    queue_own = pltpu.make_async_copy(queue_ref, ZA, own_sem.at[1])
    queue_own.start()
    last = f == F - 1
    noise_own = lambda: pltpu.make_async_copy(
        noise_ref, ZB.at[pl.ds(half, half), :], own_sem.at[2]
    )
    guarded(last, lambda: noise_own().start())
    for s in range(2):

        @pl.when(f == 0)
        def _(s=s):
            KB[s, :T] = jnp.zeros((T, inner), BF16)
            VB[s, :T] = jnp.zeros((T, inner), BF16)

        @pl.when(last)
        def _(s=s):
            KB[s, 2 * T :] = jnp.zeros((T, inner), BF16)
            VB[s, 2 * T :] = jnp.zeros((T, inner), BF16)

    def tables():
        lane = lax.broadcasted_iota(jnp.int32, (1, HEAD_SIZE), 1)
        sign = jnp.where(lane < HEAD_SIZE // 2, -1.0, 1.0)
        for b in range(2):
            level = level_ref[b]
            for k in range(3):
                mod_ref[b * 3 + k : b * 3 + k + 1, :] = table[k, pl.ds(level, 1), :]
            angles = freq_ref[...] * pos_ref[b].astype(F32)
            rows = slice(b * half, (b + 1) * half)
            cos_ref[rows, :] = jnp.broadcast_to(jnp.cos(angles), (half, HEAD_SIZE))
            sin_ref[rows, :] = jnp.broadcast_to(jnp.sin(angles) * sign, (half, HEAD_SIZE))

    def sigma_step(b):
        return sigma_ref[level_ref[b] + 1] - sigma_ref[level_ref[b]]

    def modulate(s, src):
        rows = 16
        low_lanes = lax.broadcasted_iota(jnp.int32, (rows, 128), 1) < 64

        def measure(i, carry):
            at = pl.ds(pl.multiple_of(i * rows, rows), rows)
            wide = src[at, :].astype(F32)
            mean = jnp.mean(wide, axis=-1, keepdims=True)
            wide = wide - mean
            square = jnp.sum(wide * wide, axis=-1, keepdims=True)
            ST[s, h, at, :] = jnp.where(low_lanes, mean, square)
            return carry

        lax.fori_loop(0, T // rows, measure, 0)
        for step in range(1, H):
            send(ST.at[s, h], ST.at[s, h], st_send.at[s, step], st_recv.at[s, h], f, head_at(step))
        for step in range(1, H):
            g = head_at(step)
            arrived(ST.at[s, g], st_recv.at[s, g])
        for b in range(2):
            shift = mod_ref[b * 3 : b * 3 + 1, :]
            scale = 1.0 + mod_ref[b * 3 + 1 : b * 3 + 2, :]

            def body(i, carry, b=b, shift=shift, scale=scale):
                at = pl.ds(pl.multiple_of(b * half + i * rows, rows), rows)
                stats = [ST[s, g, at, :] for g in range(H)]
                means = [one[:, 0:1] for one in stats]
                mean = sum(means) / H
                square = sum(one[:, 64:65] for one in stats)
                square = square + slab * sum((one - mean) * (one - mean) for one in means)
                scale_by = lax.rsqrt(square / (H * slab) + 1e-06)
                MOD[at, :] = (
                    (src[at, :].astype(F32) - mean) * scale_by * scale + shift
                ).astype(BF16)
                return carry

            lax.fori_loop(0, half // rows, body, 0)

    depth = 1280 if slab % 1280 == 0 else slab

    def project(s, m):
        for step in list(range(1, H)) + [0]:
            g = head_at(step)

            def body(i, acc, g=g):
                at = pl.multiple_of(i * depth, 128)
                return acc + jnp.dot(
                    MOD[:, pl.ds(at, depth)],
                    W[m, g, pl.ds(at, depth), :],
                    preferred_element_type=F32,
                )

            total = lax.fori_loop(0, slab // depth, body, jnp.zeros((T, inner), F32))
            if step == 0:
                PO[m] = total
                continue
            PS[s, m, step] = total.astype(BF16)
            send(
                PS.at[s, m, step],
                PR.at[s, m, h],
                p_send.at[s, m, step],
                p_recv.at[s, m, h],
                f,
                g,
            )

    def summed(s, m):
        total = PO[m]
        for step in range(1, H):
            g = head_at(step)
            arrived(PR.at[s, m, g], p_recv.at[s, m, g])
            total = total + PR[s, m, g].astype(F32)
        return total

    def rotated(full):
        parts = []
        for i in range(heads):
            one = full[:, i * HEAD_SIZE : (i + 1) * HEAD_SIZE]
            one = one * lax.rsqrt(jnp.mean(one * one, axis=-1, keepdims=True) + 1e-06)
            turned = pltpu.roll(one, HEAD_SIZE // 2, 1)
            parts.append((one * cos_ref[...] + turned * sin_ref[...]).astype(BF16))
        return parts

    def keys(s):
        for i, part in enumerate(rotated(summed(s, 0))):
            KB[s, T : 2 * T, i * HEAD_SIZE : (i + 1) * HEAD_SIZE] = part
        halo(KB, s, k_send, k_recv)

    def values(s):
        VB[s, T : 2 * T, :] = summed(s, 1).astype(BF16)
        halo(VB, s, v_send, v_recv)

    def halo(buf, s, ssem, rsem):
        mid = buf.at[s, pl.ds(T, T), :]
        send(mid, buf.at[s, pl.ds(0, T), :], ssem.at[s, 0], rsem.at[s, 0], f + 1, h, when=f < F - 1)
        send(mid, buf.at[s, pl.ds(2 * T, T), :], ssem.at[s, 1], rsem.at[s, 1], f - 1, h, when=f > 0)

    def queries(s):
        for i, part in enumerate(rotated(summed(s, 2))):
            QB[:, i * HEAD_SIZE : (i + 1) * HEAD_SIZE] = part

    def attend(s):
        for buf, rsem in ((KB, k_recv), (VB, v_recv)):
            arrived(buf.at[s, pl.ds(0, T), :], rsem.at[s, 0], when=f > 0)
            arrived(buf.at[s, pl.ds(2 * T, T), :], rsem.at[s, 1], when=f < F - 1)
        shape = (T, 3 * T)
        qb = lax.broadcasted_iota(jnp.int32, shape, 0) // half
        kb = lax.broadcasted_iota(jnp.int32, shape, 1) // half - 2
        near = (kb - qb <= REACH) & (qb - kb <= REACH)
        near = near & (kb + 2 * f >= 0) & (kb + 2 * f < 2 * F)
        for i in range(heads):
            cols = slice(i * HEAD_SIZE, (i + 1) * HEAD_SIZE)
            scores = lax.dot_general(
                QB[:, cols], KB[s, :, cols], (((1,), (1,)), ((), ())), preferred_element_type=F32
            )
            raised = jnp.where(near, jnp.exp(scores * (1.0 / math.sqrt(HEAD_SIZE))), 0.0)
            weights = raised / jnp.sum(raised, axis=-1, keepdims=True)
            ATT[s, h, :, cols] = jnp.dot(
                weights.astype(BF16), VB[s, :, cols], preferred_element_type=F32
            ).astype(BF16)
        for step in range(1, H):
            send(ATT.at[s, h], ATT.at[s, h], t_send.at[s, step], t_recv.at[s, h], f, head_at(step))

    def attended_all(s):
        for step in range(1, H):
            g = head_at(step)
            arrived(ATT.at[s, g], t_recv.at[s, g])

    def advance(s, src):
        for n in range(chunks):
            cols = slice(n * NC, (n + 1) * NC)
            mixed = None
            for g in range(H):
                product = lax.dot_general(
                    ATT[s, g],
                    W[3, g, cols, :],
                    (((1,), (1,)), ((), ())),
                    preferred_element_type=F32,
                )
                product = product.astype(BF16).astype(F32)
                mixed = product if mixed is None else mixed + product
            for b in range(2):
                rows = slice(b * half, (b + 1) * half)
                base = src[rows, cols].astype(F32)
                gate = mod_ref[b * 3 + 2 : b * 3 + 3, cols]
                layer_out = base + gate * mixed[rows]
                following = (base + sigma_step(b) * layer_out).astype(BF16)
                if s == 1:
                    vel_ref[rows, cols] = layer_out.astype(BF16)
                    out_ref[rows, cols] = following
                elif b == 0:
                    NX[:, cols] = following
                else:
                    ZB[:half, cols] = following
            if s == 0:
                at = pl.ds(n * NC, NC)
                send(
                    NX.at[:, at],
                    ZB.at[pl.ds(half, half), at],
                    b_send.at[n],
                    b_recv.at[n],
                    f - 1,
                    h,
                    when=f > 0,
                )

    def second_state():
        for n in range(chunks):
            at = pl.ds(n * NC, NC)
            arrived(ZB.at[pl.ds(half, half), at], b_recv.at[n], when=f < F - 1)
        guarded(last, lambda: noise_own().wait())

    w_along(0, 1)
    w_own(1)
    for d in range(2, Z):
        w_along(0, d)
    w_heads(0)
    w_along(1, 1)
    queue_own.wait()
    table_own.wait()
    tables()
    modulate(0, ZA)
    w_across(0)
    w_own(2)
    for d in range(2, Z):
        w_along(1, d)
    w_heads(1)
    w_last(0)
    project(0, 0)
    w_along(2, 1)
    w_across(1)
    w_own(3)
    for d in range(2, Z):
        w_along(2, d)
    w_heads(2)
    w_last(1)
    project(0, 1)
    w_along(3, 1)
    keys(0)
    w_across(2)
    for d in range(2, Z):
        w_along(3, d)
    w_heads(3)
    w_last(2)
    project(0, 2)
    values(0)
    queries(0)
    attend(0)
    w_across(3)
    w_last(3)
    attended_all(0)
    advance(0, ZA)
    second_state()
    modulate(1, ZB)
    project(1, 0)
    project(1, 1)
    keys(1)
    project(1, 2)
    values(1)
    queries(1)
    attend(1)
    attended_all(1)
    advance(1, ZB)
    for when, action in pending:
        guarded(when, action)


def per_device(
    queue,
    noise_block,
    w_query,
    w_key,
    w_value,
    w_output,
    mod_table,
    sigma_table,
    timestep_index,
    block_position,
):
    F = lax.axis_size("frame")
    H = lax.axis_size("head")
    T, slab = queue.shape
    blocks = timestep_index.shape[0]
    half = T // blocks
    levels = mod_table.shape[0]
    R, inner = w_key.shape
    Z = F // 4
    zs = Z // H
    chunks = slab // 640
    freqs = 10000.0 ** (-np.arange(HEAD_SIZE // 2) / (HEAD_SIZE // 2))
    freqs = jnp.asarray(np.concatenate([freqs, freqs])[None, :].astype(np.float32))
    dma = pltpu.SemaphoreType.DMA
    vmem = pl.BlockSpec(memory_space=pltpu.VMEM)
    smem = pl.BlockSpec(memory_space=pltpu.SMEM)
    hbm = pl.BlockSpec(memory_space=pl.ANY)
    out = jax.ShapeDtypeStruct((T, slab), BF16)
    return pl.pallas_call(
        functools.partial(kernel, F, H),
        out_shape=(out, out),
        in_specs=[hbm] * 7 + [vmem] + [smem] * 3,
        out_specs=(vmem, vmem),
        scratch_shapes=[
            pltpu.VMEM((4, H, slab, inner), BF16),
            pltpu.VMEM((4, Z, R, inner), BF16),
            pltpu.VMEM((T, slab), BF16),
            pltpu.VMEM((T, slab), BF16),
            pltpu.VMEM((T, slab), BF16),
            pltpu.VMEM((half, slab), BF16),
            pltpu.VMEM((T, inner), BF16),
            pltpu.VMEM((2, 3 * T, inner), BF16),
            pltpu.VMEM((2, 3 * T, inner), BF16),
            pltpu.VMEM((2, H, T, inner), BF16),
            pltpu.VMEM((3, T, inner), F32),
            pltpu.VMEM((2, 3, H, T, inner), BF16),
            pltpu.VMEM((2, 3, H, T, inner), BF16),
            pltpu.VMEM((2, H, T, 128), F32),
            pltpu.VMEM((3, levels, slab), F32),
            pltpu.VMEM((blocks * 3, slab), F32),
            pltpu.VMEM((T, HEAD_SIZE), F32),
            pltpu.VMEM((T, HEAD_SIZE), F32),
            dma((3,)),
            dma((4, Z)),
            dma((4, Z)),
            dma((4, Z)),
            dma((4, Z)),
            dma((4, H, zs)),
            dma((4, H, zs)),
            dma((4, H, zs)),
            dma((4, H, zs, 2)),
            dma((4, H, zs, 2)),
            dma((4, zs)),
            dma((chunks,)),
            dma((chunks,)),
            dma((2, 2)),
            dma((2, 2)),
            dma((2, 2)),
            dma((2, 2)),
            dma((2, H)),
            dma((2, H)),
            dma((2, 3, H)),
            dma((2, 3, H)),
            dma((2, H)),
            dma((2, H)),
        ],
        compiler_params=pltpu.CompilerParams(
            collective_id=0, has_side_effects=True, vmem_limit_bytes=62 * 1024 * 1024
        ),
        cost_estimate=pl.CostEstimate(
            flops=4 * T * H * slab * inner * 4, bytes_accessed=8 * R * inner * 2, transcendentals=0
        ),
    )(
        queue,
        noise_block,
        w_key,
        w_value,
        w_query,
        w_output.T,
        jnp.transpose(mod_table, (1, 0, 2)),
        freqs,
        sigma_table,
        timestep_index,
        block_position,
    )


def solution(mesh):
    in_specs = (
        P("frame", "head"),
        P(None, "head"),
        P("frame", "head"),
        P("frame", "head"),
        P("frame", "head"),
        P("head", "frame"),
        P(),
        P(),
        P("frame"),
        P("frame"),
    )
    out_specs = (P("frame", "head"), P("frame", "head"))
    return jax.shard_map(
        per_device, mesh=mesh, in_specs=in_specs, out_specs=out_specs, check_vma=False
    )
```

```python
import functools
import math

import jax
import jax.numpy as jnp
import numpy as np
from jax import lax
from jax.experimental import pallas as pl
from jax.experimental.pallas import tpu as pltpu
from jax.sharding import PartitionSpec as P

HEAD_SIZE = 128
REACH = 2
MESH = pl.DeviceIdType.MESH
F32 = jnp.float32
BF16 = jnp.bfloat16


def kernel(
    F,
    H,
    queue_ref,
    noise_ref,
    wk_ref,
    wv_ref,
    wq_ref,
    wo_ref,
    table_ref,
    freq_ref,
    sigma_ref,
    level_ref,
    pos_ref,
    vel_ref,
    out_ref,
    W,
    ZL,
    ZA,
    ZB,
    MOD,
    NX,
    QB,
    KB,
    VB,
    ATT,
    PO,
    PS,
    PR,
    ST,
    table,
    mod_ref,
    cos_ref,
    sin_ref,
    own_sem,
    z_recv,
    z_up,
    z_dn,
    y_send,
    y_recv,
    x_send,
    x_recv,
    s_send,
    s_recv,
    l_sem,
    e_up,
    e_dn,
    e_recv,
    b_recv,
    b_send,
    k_recv,
    k_send,
    v_recv,
    v_send,
    t_recv,
    t_send,
    p_recv,
    p_send,
    st_recv,
    st_send,
):
    f = lax.axis_index("frame")
    h = lax.axis_index("head")
    Z = F // 4
    zs = Z // H
    z = f // 4
    x = (f // 2) % 2
    c = f % 2
    R, inner = wk_ref.shape
    T, slab = queue_ref.shape
    half = T // 2
    NC = 640
    chunks = slab // NC
    heads = inner // HEAD_SIZE
    pending = []

    def fid(zz, xx, cc):
        return (zz * 2 + xx) * 2 + cc

    def head_at(step):
        return (h + step) % H

    def send(src, dst, ssem, rsem, to_f, to_h, when=None):
        def make():
            return pltpu.make_async_remote_copy(
                src_ref=src,
                dst_ref=dst,
                send_sem=ssem,
                recv_sem=rsem,
                device_id=(to_f, to_h),
                device_id_type=MESH,
            )

        guarded(when, lambda: make().start())
        pending.append((when, lambda: make().wait_send()))

    def guarded(when, action):
        if when is None:
            action()
        else:
            pl.when(when)(action)

    def arrived(dst, rsem, when=None):
        guarded(
            when,
            lambda: pltpu.make_async_remote_copy(
                src_ref=dst,
                dst_ref=dst,
                send_sem=rsem,
                recv_sem=rsem,
                device_id=(fid(z, x, 1 - c), h),
                device_id_type=MESH,
            ).wait_recv(),
        )

    barrier = pltpu.get_barrier_semaphore()
    greet = [
        (z < Z - 1, f + 4, h),
        (z > 0, f - 4, h),
        (None, fid(z, 1 - x, c), h),
        (None, fid(z, x, 1 - c), h),
        (f < F - 1, f + 1, h),
        (f > 0, f - 1, h),
    ]
    for step in range(1, H):
        greet.append((None, f, head_at(step)))
    for when, to_f, to_h in greet:
        guarded(
            when,
            lambda to_f=to_f, to_h=to_h: pl.semaphore_signal(
                barrier, inc=1, device_id=(to_f, to_h), device_id_type=MESH
            ),
        )
    always = sum(when is None for when, _, _ in greet)
    sometimes = sum(when.astype(jnp.int32) for when, _, _ in greet if when is not None)
    pl.semaphore_wait(barrier, always + sometimes)

    shards = [wk_ref, wv_ref, wq_ref, wo_ref]

    def slot(m, g, j, xx, cc):
        return W.at[m, g, pl.ds(pl.multiple_of(fid(j, xx, cc) * R, 32), R), :]

    along_z = (1, 3) if zs <= 2 else ()
    in_slab = z // zs == h
    above, below = z >= (h + 1) * zs, z < h * zs
    rank = z - h * zs
    extra = jnp.where(in_slab, 1 - rank, jnp.where(above, zs - 1, 0))
    has_extra = (zs == 2) | jnp.logical_not(in_slab)

    def both(one, other):
        return other if one is None else one & other

    def local(m, zz, src):
        j = zz - zz // zs * zs
        return pltpu.make_async_copy(src, slot(m, h, j, x, c), l_sem.at[m, j])

    def pass_on(m, g, j, src, when=None, own_group=False):
        dst = slot(m, g, j, x, c)
        across = both(when, j != extra) if own_group and m in along_z else when
        send(src, dst, x_send.at[m, g, j], x_recv.at[m, g, j], fid(z, 1 - x, c), h, when=across)
        send(
            src, dst, s_send.at[m, g, j, x], s_recv.at[m, g, j, x], fid(z, x, 1 - c), h, when=when
        )

    def hand_out(m, zz, src, when=None):
        home = zz // zs
        j = zz - home * zs
        used = both(when, home == h)
        guarded(used, lambda: local(m, zz, src).start())
        pass_on(m, h, j, src, when=used, own_group=True)
        send(
            src,
            slot(m, h, j, x, c),
            y_send.at[m, zz],
            y_recv.at[m, h, j],
            f,
            home,
            when=both(when, home != h),
        )

    def w_own(m):
        src = shards[m]
        send(src, ZL.at[m, z], z_up.at[m, z], z_recv.at[m, z], f + 4, h, when=z < Z - 1)
        send(src, ZL.at[m, z], z_dn.at[m, z], z_recv.at[m, z], f - 4, h, when=z > 0)
        hand_out(m, z, src)

    def w_along(m, d):
        for zz, ok, up in ((z - d, z - d >= 0, True), (z + d, z + d <= Z - 1, False)):
            piece = ZL.at[m, zz]
            arrived(piece, z_recv.at[m, zz], when=ok)
            if up:
                send(piece, piece, z_up.at[m, zz], z_recv.at[m, zz], f + 4, h, when=ok & (z < Z - 1))
            else:
                send(piece, piece, z_dn.at[m, zz], z_recv.at[m, zz], f - 4, h, when=ok & (z > 0))
            hand_out(m, zz, piece, when=ok)

    def turns():
        for i in range(zs):
            yield jnp.where(z <= h * zs, i, zs - 1 - i)

    def w_heads(m):
        for j in turns():
            for step in range(1, H):
                g = head_at(step)
                piece = slot(m, g, j, x, c)
                arrived(piece, y_recv.at[m, g, j])
                pass_on(m, g, j, piece)

    def to_sibling(m, g, j, piece, when=None):
        send(
            piece,
            piece,
            s_send.at[m, g, j, 1 - x],
            s_recv.at[m, g, j, 1 - x],
            fid(z, x, 1 - c),
            h,
            when=when,
        )

    def along(m, piece, up, down):
        send(piece, piece, e_up.at[m], e_recv.at[m], f + 4, h, when=up & (z < Z - 1))
        send(piece, piece, e_dn.at[m], e_recv.at[m], f - 4, h, when=down & (z > 0))

    def w_swap(m):
        piece = slot(m, h, rank, 1 - x, c)
        arrived(piece, x_recv.at[m, h, rank], when=in_slab)
        to_sibling(m, h, rank, piece, when=in_slab)
        if m in along_z:
            along(m, piece, in_slab, in_slab)

    def w_extra(m):
        if m in along_z:
            piece = slot(m, h, extra, 1 - x, c)
            arrived(piece, e_recv.at[m], when=has_extra)
            to_sibling(m, h, extra, piece, when=has_extra)
            along(m, piece, above, below)

    def w_across(m):
        for j in turns():
            for step in range(H):
                g = head_at(step)
                rest = None
                if step == 0:
                    rest = jnp.logical_not(in_slab & (j == rank))
                    if m in along_z:
                        rest = rest & (j != extra)
                piece = slot(m, g, j, 1 - x, c)
                arrived(piece, x_recv.at[m, g, j], when=rest)
                to_sibling(m, g, j, piece, when=rest)

    def w_last(m):
        for j in range(zs):
            for g in range(H):
                for xx in range(2):
                    arrived(slot(m, g, j, xx, 1 - c), s_recv.at[m, g, j, xx])
            local(m, h * zs + j, shards[m]).wait()

    queue_own = pltpu.make_async_copy(queue_ref, ZA, own_sem.at[1])
    queue_own.start()
    w_own(0)
    w_own(1)
    table_own = pltpu.make_async_copy(
        table_ref.at[:, :, pl.ds(pl.multiple_of(h * slab, 128), slab)], table, own_sem.at[0]
    )
    table_own.start()
    last = f == F - 1
    noise_own = lambda: pltpu.make_async_copy(
        noise_ref, ZB.at[pl.ds(half, half), :], own_sem.at[2]
    )
    guarded(last, lambda: noise_own().start())
    for s in range(2):

        @pl.when(f == 0)
        def _(s=s):
            KB[s, :T] = jnp.zeros((T, inner), BF16)
            VB[s, :T] = jnp.zeros((T, inner), BF16)

        @pl.when(last)
        def _(s=s):
            KB[s, 2 * T :] = jnp.zeros((T, inner), BF16)
            VB[s, 2 * T :] = jnp.zeros((T, inner), BF16)

    def tables():
        lane = lax.broadcasted_iota(jnp.int32, (1, HEAD_SIZE), 1)
        sign = jnp.where(lane < HEAD_SIZE // 2, -1.0, 1.0)
        for b in range(2):
            level = level_ref[b]
            for k in range(3):
                mod_ref[b * 3 + k : b * 3 + k + 1, :] = table[k, pl.ds(level, 1), :]
            angles = freq_ref[...] * pos_ref[b].astype(F32)
            rows = slice(b * half, (b + 1) * half)
            cos_ref[rows, :] = jnp.broadcast_to(jnp.cos(angles), (half, HEAD_SIZE))
            sin_ref[rows, :] = jnp.broadcast_to(jnp.sin(angles) * sign, (half, HEAD_SIZE))

    def sigma_step(b):
        return sigma_ref[level_ref[b] + 1] - sigma_ref[level_ref[b]]

    def measure_rows(s, src):
        rows = 16
        low_lanes = lax.broadcasted_iota(jnp.int32, (rows, 128), 1) < 64

        def measure(i, carry):
            at = pl.ds(pl.multiple_of(i * rows, rows), rows)
            wide = src[at, :].astype(F32)
            mean = jnp.mean(wide, axis=-1, keepdims=True)
            wide = wide - mean
            square = jnp.sum(wide * wide, axis=-1, keepdims=True)
            ST[s, h, at, :] = jnp.where(low_lanes, mean, square)
            return carry

        lax.fori_loop(0, T // rows, measure, 0)
        for step in range(1, H):
            send(ST.at[s, h], ST.at[s, h], st_send.at[s, step], st_recv.at[s, h], f, head_at(step))

    def modulate(s, src):
        rows = 16
        for step in range(1, H):
            g = head_at(step)
            arrived(ST.at[s, g], st_recv.at[s, g])
        for b in range(2):
            shift = mod_ref[b * 3 : b * 3 + 1, :]
            scale = 1.0 + mod_ref[b * 3 + 1 : b * 3 + 2, :]

            def body(i, carry, b=b, shift=shift, scale=scale):
                at = pl.ds(pl.multiple_of(b * half + i * rows, rows), rows)
                stats = [ST[s, g, at, :] for g in range(H)]
                means = [one[:, 0:1] for one in stats]
                mean = sum(means) / H
                square = sum(one[:, 64:65] for one in stats)
                square = square + slab * sum((one - mean) * (one - mean) for one in means)
                scale_by = lax.rsqrt(square / (H * slab) + 1e-06)
                MOD[at, :] = (
                    (src[at, :].astype(F32) - mean) * scale_by * scale + shift
                ).astype(BF16)
                return carry

            lax.fori_loop(0, half // rows, body, 0)

    depth = 1280 if slab % 1280 == 0 else slab

    def project(s, m):
        for step in list(range(1, H)) + [0]:
            g = head_at(step)

            def body(i, acc, g=g):
                at = pl.multiple_of(i * depth, 128)
                return acc + jnp.dot(
                    MOD[:, pl.ds(at, depth)],
                    W[m, g, pl.ds(at, depth), :],
                    preferred_element_type=F32,
                )

            total = lax.fori_loop(0, slab // depth, body, jnp.zeros((T, inner), F32))
            if step == 0:
                PO[m] = total
                continue
            PS[s, m, step] = total.astype(BF16)
            send(
                PS.at[s, m, step],
                PR.at[s, m, h],
                p_send.at[s, m, step],
                p_recv.at[s, m, h],
                f,
                g,
            )

    def summed(s, m):
        total = PO[m]
        for step in range(1, H):
            g = head_at(step)
            arrived(PR.at[s, m, g], p_recv.at[s, m, g])
            total = total + PR[s, m, g].astype(F32)
        return total

    def rotated(full):
        parts = []
        for i in range(heads):
            one = full[:, i * HEAD_SIZE : (i + 1) * HEAD_SIZE]
            one = one * lax.rsqrt(jnp.mean(one * one, axis=-1, keepdims=True) + 1e-06)
            turned = pltpu.roll(one, HEAD_SIZE // 2, 1)
            parts.append((one * cos_ref[...] + turned * sin_ref[...]).astype(BF16))
        return parts

    def keys(s):
        for i, part in enumerate(rotated(summed(s, 0))):
            KB[s, T : 2 * T, i * HEAD_SIZE : (i + 1) * HEAD_SIZE] = part
        halo(KB, s, k_send, k_recv)

    def values(s):
        VB[s, T : 2 * T, :] = summed(s, 1).astype(BF16)
        halo(VB, s, v_send, v_recv)

    def halo(buf, s, ssem, rsem):
        mid = buf.at[s, pl.ds(T, T), :]
        send(mid, buf.at[s, pl.ds(0, T), :], ssem.at[s, 0], rsem.at[s, 0], f + 1, h, when=f < F - 1)
        send(mid, buf.at[s, pl.ds(2 * T, T), :], ssem.at[s, 1], rsem.at[s, 1], f - 1, h, when=f > 0)

    def queries(s):
        for i, part in enumerate(rotated(summed(s, 2))):
            QB[:, i * HEAD_SIZE : (i + 1) * HEAD_SIZE] = part

    def attend(s):
        for buf, rsem in ((KB, k_recv), (VB, v_recv)):
            arrived(buf.at[s, pl.ds(0, T), :], rsem.at[s, 0], when=f > 0)
            arrived(buf.at[s, pl.ds(2 * T, T), :], rsem.at[s, 1], when=f < F - 1)
        shape = (T, 3 * T)
        qb = lax.broadcasted_iota(jnp.int32, shape, 0) // half
        kb = lax.broadcasted_iota(jnp.int32, shape, 1) // half - 2
        near = (kb - qb <= REACH) & (qb - kb <= REACH)
        near = near & (kb + 2 * f >= 0) & (kb + 2 * f < 2 * F)
        for i in range(heads):
            cols = slice(i * HEAD_SIZE, (i + 1) * HEAD_SIZE)
            scores = lax.dot_general(
                QB[:, cols], KB[s, :, cols], (((1,), (1,)), ((), ())), preferred_element_type=F32
            )
            raised = jnp.where(near, jnp.exp(scores * (1.0 / math.sqrt(HEAD_SIZE))), 0.0)
            weights = raised / jnp.sum(raised, axis=-1, keepdims=True)
            ATT[s, h, :, cols] = jnp.dot(
                weights.astype(BF16), VB[s, :, cols], preferred_element_type=F32
            ).astype(BF16)
        for step in range(1, H):
            send(ATT.at[s, h], ATT.at[s, h], t_send.at[s, step], t_recv.at[s, h], f, head_at(step))

    def attended_all(s):
        for step in range(1, H):
            g = head_at(step)
            arrived(ATT.at[s, g], t_recv.at[s, g])

    def advance(s, src):
        for n in range(chunks):
            cols = slice(n * NC, (n + 1) * NC)
            mixed = None
            for g in range(H):
                product = lax.dot_general(
                    ATT[s, g],
                    W[3, g, cols, :],
                    (((1,), (1,)), ((), ())),
                    preferred_element_type=F32,
                )
                product = product.astype(BF16).astype(F32)
                mixed = product if mixed is None else mixed + product
            for b in range(2):
                rows = slice(b * half, (b + 1) * half)
                base = src[rows, cols].astype(F32)
                gate = mod_ref[b * 3 + 2 : b * 3 + 3, cols]
                layer_out = base + gate * mixed[rows]
                following = (base + sigma_step(b) * layer_out).astype(BF16)
                if s == 1:
                    vel_ref[rows, cols] = layer_out.astype(BF16)
                    out_ref[rows, cols] = following
                elif b == 0:
                    NX[:, cols] = following
                else:
                    ZB[:half, cols] = following
            if s == 0:
                at = pl.ds(n * NC, NC)
                send(
                    NX.at[:, at],
                    ZB.at[pl.ds(half, half), at],
                    b_send.at[n],
                    b_recv.at[n],
                    f - 1,
                    h,
                    when=f > 0,
                )

    def second_state():
        for n in range(chunks):
            at = pl.ds(n * NC, NC)
            arrived(ZB.at[pl.ds(half, half), at], b_recv.at[n], when=f < F - 1)
        guarded(last, lambda: noise_own().wait())

    queue_own.wait()
    measure_rows(0, ZA)
    w_along(0, 1)
    w_swap(0)
    for d in range(2, Z):
        w_along(0, d)
    w_heads(0)
    w_along(1, 1)
    w_swap(1)
    w_across(0)
    w_own(2)
    for d in range(2, Z):
        w_along(1, d)
    w_heads(1)
    w_extra(1)
    w_along(2, 1)
    w_swap(2)
    table_own.wait()
    tables()
    modulate(0, ZA)
    w_last(0)
    project(0, 0)
    w_across(1)
    w_own(3)
    for d in range(2, Z):
        w_along(2, d)
    w_heads(2)
    w_along(3, 1)
    w_swap(3)
    w_last(1)
    project(0, 1)
    keys(0)
    for d in range(2, Z):
        w_along(3, d)
    w_across(2)
    w_heads(3)
    w_extra(3)
    w_last(2)
    project(0, 2)
    values(0)
    queries(0)
    attend(0)
    w_across(3)
    w_last(3)
    attended_all(0)
    advance(0, ZA)
    second_state()
    measure_rows(1, ZB)
    modulate(1, ZB)
    project(1, 0)
    project(1, 1)
    keys(1)
    project(1, 2)
    values(1)
    queries(1)
    attend(1)
    attended_all(1)
    advance(1, ZB)
    for when, action in pending:
        guarded(when, action)


def per_device(
    queue,
    noise_block,
    w_query,
    w_key,
    w_value,
    w_output,
    mod_table,
    sigma_table,
    timestep_index,
    block_position,
):
    F = lax.axis_size("frame")
    H = lax.axis_size("head")
    T, slab = queue.shape
    blocks = timestep_index.shape[0]
    half = T // blocks
    levels = mod_table.shape[0]
    R, inner = w_key.shape
    Z = F // 4
    zs = Z // H
    chunks = slab // 640
    freqs = 10000.0 ** (-np.arange(HEAD_SIZE // 2) / (HEAD_SIZE // 2))
    freqs = jnp.asarray(np.concatenate([freqs, freqs])[None, :].astype(np.float32))
    dma = pltpu.SemaphoreType.DMA
    vmem = pl.BlockSpec(memory_space=pltpu.VMEM)
    smem = pl.BlockSpec(memory_space=pltpu.SMEM)
    hbm = pl.BlockSpec(memory_space=pl.ANY)
    out = pltpu.VMEM((T, slab), BF16)
    return pl.pallas_call(
        functools.partial(kernel, F, H),
        out_shape=(out, out),
        in_specs=[hbm] * 7 + [vmem] + [smem] * 3,
        out_specs=(vmem, vmem),
        scratch_shapes=[
            pltpu.VMEM((4, H, slab, inner), BF16),
            pltpu.VMEM((4, Z, R, inner), BF16),
            pltpu.VMEM((T, slab), BF16),
            pltpu.VMEM((T, slab), BF16),
            pltpu.VMEM((T, slab), BF16),
            pltpu.VMEM((half, slab), BF16),
            pltpu.VMEM((T, inner), BF16),
            pltpu.VMEM((2, 3 * T, inner), BF16),
            pltpu.VMEM((2, 3 * T, inner), BF16),
            pltpu.VMEM((2, H, T, inner), BF16),
            pltpu.VMEM((3, T, inner), F32),
            pltpu.VMEM((2, 3, H, T, inner), BF16),
            pltpu.VMEM((2, 3, H, T, inner), BF16),
            pltpu.VMEM((2, H, T, 128), F32),
            pltpu.VMEM((3, levels, slab), F32),
            pltpu.VMEM((blocks * 3, slab), F32),
            pltpu.VMEM((T, HEAD_SIZE), F32),
            pltpu.VMEM((T, HEAD_SIZE), F32),
            dma((3,)),
            dma((4, Z)),
            dma((4, Z)),
            dma((4, Z)),
            dma((4, Z)),
            dma((4, H, zs)),
            dma((4, H, zs)),
            dma((4, H, zs)),
            dma((4, H, zs, 2)),
            dma((4, H, zs, 2)),
            dma((4, zs)),
            dma((4,)),
            dma((4,)),
            dma((4,)),
            dma((chunks,)),
            dma((chunks,)),
            dma((2, 2)),
            dma((2, 2)),
            dma((2, 2)),
            dma((2, 2)),
            dma((2, H)),
            dma((2, H)),
            dma((2, 3, H)),
            dma((2, 3, H)),
            dma((2, H)),
            dma((2, H)),
        ],
        compiler_params=pltpu.CompilerParams(
            collective_id=0, has_side_effects=True, vmem_limit_bytes=62 * 1024 * 1024
        ),
        cost_estimate=pl.CostEstimate(
            flops=4 * T * H * slab * inner * 4, bytes_accessed=8 * R * inner * 2, transcendentals=0
        ),
    )(
        queue,
        noise_block,
        w_key,
        w_value,
        w_query,
        w_output.T,
        jnp.transpose(mod_table, (1, 0, 2)),
        freqs,
        sigma_table,
        timestep_index,
        block_position,
    )


def solution(mesh):
    in_specs = (
        P("frame", "head"),
        P(None, "head"),
        P("frame", "head"),
        P("frame", "head"),
        P("frame", "head"),
        P("head", "frame"),
        P(),
        P(),
        P("frame"),
        P("frame"),
    )
    out_specs = (P("frame", "head"), P("frame", "head"))
    return jax.shard_map(
        per_device, mesh=mesh, in_specs=in_specs, out_specs=out_specs, check_vma=False
    )
```

```python
import functools
import math

import jax
import jax.numpy as jnp
import numpy as np
from jax import lax
from jax.experimental import pallas as pl
from jax.experimental.pallas import tpu as pltpu
from jax.sharding import PartitionSpec as P

HEAD_SIZE = 128
REACH = 2
MESH = pl.DeviceIdType.MESH
F32 = jnp.float32
BF16 = jnp.bfloat16


def kernel(
    F,
    H,
    queue_ref,
    noise_ref,
    wk_ref,
    wv_ref,
    wq_ref,
    wo_ref,
    table_ref,
    freq_ref,
    sigma_ref,
    level_ref,
    pos_ref,
    vel_ref,
    out_ref,
    W,
    ZL,
    ZA,
    ZB,
    MOD,
    NX,
    QB,
    KB,
    VB,
    ATT,
    PO,
    PS,
    PR,
    ST,
    table,
    mod_ref,
    cos_ref,
    sin_ref,
    own_sem,
    z_recv,
    z_up,
    z_dn,
    y_send,
    y_recv,
    x_send,
    x_recv,
    s_send,
    s_recv,
    l_sem,
    e_up,
    e_dn,
    e_recv,
    b_recv,
    b_send,
    k_recv,
    k_send,
    v_recv,
    v_send,
    t_recv,
    t_send,
    p_recv,
    p_send,
    st_recv,
    st_send,
):
    f = lax.axis_index("frame")
    h = lax.axis_index("head")
    Z = F // 4
    zs = Z // H
    z = f // 4
    x = (f // 2) % 2
    c = f % 2
    R, inner = wk_ref.shape
    T, slab = queue_ref.shape
    half = T // 2
    NC = 640
    chunks = slab // NC
    heads = inner // HEAD_SIZE
    pending = []

    def fid(zz, xx, cc):
        return (zz * 2 + xx) * 2 + cc

    def head_at(step):
        return (h + step) % H

    def send(src, dst, ssem, rsem, to_f, to_h, when=None):
        def make():
            return pltpu.make_async_remote_copy(
                src_ref=src,
                dst_ref=dst,
                send_sem=ssem,
                recv_sem=rsem,
                device_id=(to_f, to_h),
                device_id_type=MESH,
            )

        guarded(when, lambda: make().start())
        pending.append((when, lambda: make().wait_send()))

    def guarded(when, action):
        if when is None:
            action()
        else:
            pl.when(when)(action)

    def arrived(dst, rsem, when=None):
        guarded(
            when,
            lambda: pltpu.make_async_remote_copy(
                src_ref=dst,
                dst_ref=dst,
                send_sem=rsem,
                recv_sem=rsem,
                device_id=(fid(z, x, 1 - c), h),
                device_id_type=MESH,
            ).wait_recv(),
        )

    barrier = pltpu.get_barrier_semaphore()
    greet = [
        (z < Z - 1, f + 4, h),
        (z > 0, f - 4, h),
        (None, fid(z, 1 - x, c), h),
        (None, fid(z, x, 1 - c), h),
        (f < F - 1, f + 1, h),
        (f > 0, f - 1, h),
    ]
    for step in range(1, H):
        greet.append((None, f, head_at(step)))
    for when, to_f, to_h in greet:
        guarded(
            when,
            lambda to_f=to_f, to_h=to_h: pl.semaphore_signal(
                barrier, inc=1, device_id=(to_f, to_h), device_id_type=MESH
            ),
        )
    always = sum(when is None for when, _, _ in greet)
    sometimes = sum(when.astype(jnp.int32) for when, _, _ in greet if when is not None)
    pl.semaphore_wait(barrier, always + sometimes)

    part = R // 2
    matrices = [wk_ref, wv_ref, wq_ref, wo_ref]
    shards = [ref.at[pl.ds(r * part, part), :] for ref in matrices for r in range(2)]
    M = len(shards)

    def slot(m, g, j, xx, cc):
        at = pl.multiple_of(fid(j, xx, cc) * R + m % 2 * part, 16)
        return W.at[m // 2, g, pl.ds(at, part), :]

    along_z = range(1, M, 2) if zs <= 2 else ()
    in_slab = z // zs == h
    above, below = z >= (h + 1) * zs, z < h * zs
    rank = z - h * zs
    extra = jnp.where(in_slab, 1 - rank, jnp.where(above, zs - 1, 0))
    has_extra = (zs == 2) | jnp.logical_not(in_slab)

    def both(one, other):
        return other if one is None else one & other

    def local(m, zz, src):
        j = zz - zz // zs * zs
        return pltpu.make_async_copy(src, slot(m, h, j, x, c), l_sem.at[m, j])

    def pass_on(m, g, j, src, when=None, own_group=False):
        dst = slot(m, g, j, x, c)
        across = both(when, j != extra) if own_group and m in along_z else when
        send(src, dst, x_send.at[m, g, j], x_recv.at[m, g, j], fid(z, 1 - x, c), h, when=across)
        send(
            src, dst, s_send.at[m, g, j, x], s_recv.at[m, g, j, x], fid(z, x, 1 - c), h, when=when
        )

    def hand_out(m, zz, src, when=None):
        home = zz // zs
        j = zz - home * zs
        used = both(when, home == h)
        guarded(used, lambda: local(m, zz, src).start())
        pass_on(m, h, j, src, when=used, own_group=True)
        send(
            src,
            slot(m, h, j, x, c),
            y_send.at[m, zz],
            y_recv.at[m, h, j],
            f,
            home,
            when=both(when, home != h),
        )

    def w_own(m):
        src = shards[m]
        send(src, ZL.at[m, z], z_up.at[m, z], z_recv.at[m, z], f + 4, h, when=z < Z - 1)
        send(src, ZL.at[m, z], z_dn.at[m, z], z_recv.at[m, z], f - 4, h, when=z > 0)
        hand_out(m, z, src)

    def w_along(m, d):
        for zz, ok, up in ((z - d, z - d >= 0, True), (z + d, z + d <= Z - 1, False)):
            piece = ZL.at[m, zz]
            arrived(piece, z_recv.at[m, zz], when=ok)
            if up:
                send(piece, piece, z_up.at[m, zz], z_recv.at[m, zz], f + 4, h, when=ok & (z < Z - 1))
            else:
                send(piece, piece, z_dn.at[m, zz], z_recv.at[m, zz], f - 4, h, when=ok & (z > 0))
            hand_out(m, zz, piece, when=ok)

    def turns():
        for i in range(zs):
            yield jnp.where(z <= h * zs, i, zs - 1 - i)

    def w_heads(m):
        for j in turns():
            for step in range(1, H):
                g = head_at(step)
                piece = slot(m, g, j, x, c)
                arrived(piece, y_recv.at[m, g, j])
                pass_on(m, g, j, piece)

    def to_sibling(m, g, j, piece, when=None):
        send(
            piece,
            piece,
            s_send.at[m, g, j, 1 - x],
            s_recv.at[m, g, j, 1 - x],
            fid(z, x, 1 - c),
            h,
            when=when,
        )

    def along(m, piece, up, down):
        send(piece, piece, e_up.at[m], e_recv.at[m], f + 4, h, when=up & (z < Z - 1))
        send(piece, piece, e_dn.at[m], e_recv.at[m], f - 4, h, when=down & (z > 0))

    def w_swap(m):
        piece = slot(m, h, rank, 1 - x, c)
        arrived(piece, x_recv.at[m, h, rank], when=in_slab)
        to_sibling(m, h, rank, piece, when=in_slab)
        if m in along_z:
            along(m, piece, in_slab, in_slab)

    def w_extra(m):
        if m in along_z:
            piece = slot(m, h, extra, 1 - x, c)
            arrived(piece, e_recv.at[m], when=has_extra)
            to_sibling(m, h, extra, piece, when=has_extra)
            along(m, piece, above, below)

    def w_across(m):
        for j in turns():
            for step in range(H):
                g = head_at(step)
                rest = None
                if step == 0:
                    rest = jnp.logical_not(in_slab & (j == rank))
                    if m in along_z:
                        rest = rest & (j != extra)
                piece = slot(m, g, j, 1 - x, c)
                arrived(piece, x_recv.at[m, g, j], when=rest)
                to_sibling(m, g, j, piece, when=rest)

    def w_last(m):
        for j in range(zs):
            for g in range(H):
                for xx in range(2):
                    arrived(slot(m, g, j, xx, 1 - c), s_recv.at[m, g, j, xx])
            local(m, h * zs + j, shards[m]).wait()

    queue_own = pltpu.make_async_copy(queue_ref, ZA, own_sem.at[1])
    queue_own.start()
    w_own(0)
    w_own(1)
    w_own(2)
    table_own = pltpu.make_async_copy(
        table_ref.at[:, :, pl.ds(pl.multiple_of(h * slab, 128), slab)], table, own_sem.at[0]
    )
    table_own.start()
    last = f == F - 1
    noise_own = lambda: pltpu.make_async_copy(
        noise_ref, ZB.at[pl.ds(half, half), :], own_sem.at[2]
    )
    guarded(last, lambda: noise_own().start())
    for s in range(2):

        @pl.when(f == 0)
        def _(s=s):
            KB[s, :T] = jnp.zeros((T, inner), BF16)
            VB[s, :T] = jnp.zeros((T, inner), BF16)

        @pl.when(last)
        def _(s=s):
            KB[s, 2 * T :] = jnp.zeros((T, inner), BF16)
            VB[s, 2 * T :] = jnp.zeros((T, inner), BF16)

    def tables():
        lane = lax.broadcasted_iota(jnp.int32, (1, HEAD_SIZE), 1)
        sign = jnp.where(lane < HEAD_SIZE // 2, -1.0, 1.0)
        for b in range(2):
            level = level_ref[b]
            for k in range(3):
                mod_ref[b * 3 + k : b * 3 + k + 1, :] = table[k, pl.ds(level, 1), :]
            angles = freq_ref[...] * pos_ref[b].astype(F32)
            rows = slice(b * half, (b + 1) * half)
            cos_ref[rows, :] = jnp.broadcast_to(jnp.cos(angles), (half, HEAD_SIZE))
            sin_ref[rows, :] = jnp.broadcast_to(jnp.sin(angles) * sign, (half, HEAD_SIZE))

    def sigma_step(b):
        return sigma_ref[level_ref[b] + 1] - sigma_ref[level_ref[b]]

    def measure_rows(s, src):
        rows = 16
        low_lanes = lax.broadcasted_iota(jnp.int32, (rows, 128), 1) < 64

        def measure(i, carry):
            at = pl.ds(pl.multiple_of(i * rows, rows), rows)
            wide = src[at, :].astype(F32)
            mean = jnp.mean(wide, axis=-1, keepdims=True)
            wide = wide - mean
            square = jnp.sum(wide * wide, axis=-1, keepdims=True)
            ST[s, h, at, :] = jnp.where(low_lanes, mean, square)
            return carry

        lax.fori_loop(0, T // rows, measure, 0)
        for step in range(1, H):
            send(ST.at[s, h], ST.at[s, h], st_send.at[s, step], st_recv.at[s, h], f, head_at(step))

    def modulate(s, src):
        rows = 16
        for step in range(1, H):
            g = head_at(step)
            arrived(ST.at[s, g], st_recv.at[s, g])
        for b in range(2):
            shift = mod_ref[b * 3 : b * 3 + 1, :]
            scale = 1.0 + mod_ref[b * 3 + 1 : b * 3 + 2, :]

            def body(i, carry, b=b, shift=shift, scale=scale):
                at = pl.ds(pl.multiple_of(b * half + i * rows, rows), rows)
                stats = [ST[s, g, at, :] for g in range(H)]
                means = [one[:, 0:1] for one in stats]
                mean = sum(means) / H
                square = sum(one[:, 64:65] for one in stats)
                square = square + slab * sum((one - mean) * (one - mean) for one in means)
                scale_by = lax.rsqrt(square / (H * slab) + 1e-06)
                MOD[at, :] = (
                    (src[at, :].astype(F32) - mean) * scale_by * scale + shift
                ).astype(BF16)
                return carry

            lax.fori_loop(0, half // rows, body, 0)

    depth = 1280 if slab % 1280 == 0 else slab

    def project(s, m):
        for step in list(range(1, H)) + [0]:
            g = head_at(step)

            def body(i, acc, g=g):
                at = pl.multiple_of(i * depth, 128)
                return acc + jnp.dot(
                    MOD[:, pl.ds(at, depth)],
                    W[m, g, pl.ds(at, depth), :],
                    preferred_element_type=F32,
                )

            total = lax.fori_loop(0, slab // depth, body, jnp.zeros((T, inner), F32))
            if step == 0:
                PO[m] = total
                continue
            PS[s, m, step] = total.astype(BF16)
            send(
                PS.at[s, m, step],
                PR.at[s, m, h],
                p_send.at[s, m, step],
                p_recv.at[s, m, h],
                f,
                g,
            )

    def summed(s, m):
        total = PO[m]
        for step in range(1, H):
            g = head_at(step)
            arrived(PR.at[s, m, g], p_recv.at[s, m, g])
            total = total + PR[s, m, g].astype(F32)
        return total

    def rotated(full):
        parts = []
        for i in range(heads):
            one = full[:, i * HEAD_SIZE : (i + 1) * HEAD_SIZE]
            one = one * lax.rsqrt(jnp.mean(one * one, axis=-1, keepdims=True) + 1e-06)
            turned = pltpu.roll(one, HEAD_SIZE // 2, 1)
            parts.append((one * cos_ref[...] + turned * sin_ref[...]).astype(BF16))
        return parts

    def keys(s):
        for i, part in enumerate(rotated(summed(s, 0))):
            KB[s, T : 2 * T, i * HEAD_SIZE : (i + 1) * HEAD_SIZE] = part
        halo(KB, s, k_send, k_recv)

    def values(s):
        VB[s, T : 2 * T, :] = summed(s, 1).astype(BF16)
        halo(VB, s, v_send, v_recv)

    def halo(buf, s, ssem, rsem):
        mid = buf.at[s, pl.ds(T, T), :]
        send(mid, buf.at[s, pl.ds(0, T), :], ssem.at[s, 0], rsem.at[s, 0], f + 1, h, when=f < F - 1)
        send(mid, buf.at[s, pl.ds(2 * T, T), :], ssem.at[s, 1], rsem.at[s, 1], f - 1, h, when=f > 0)

    def queries(s):
        for i, part in enumerate(rotated(summed(s, 2))):
            QB[:, i * HEAD_SIZE : (i + 1) * HEAD_SIZE] = part

    def attend(s):
        for buf, rsem in ((KB, k_recv), (VB, v_recv)):
            arrived(buf.at[s, pl.ds(0, T), :], rsem.at[s, 0], when=f > 0)
            arrived(buf.at[s, pl.ds(2 * T, T), :], rsem.at[s, 1], when=f < F - 1)
        shape = (T, 3 * T)
        qb = lax.broadcasted_iota(jnp.int32, shape, 0) // half
        kb = lax.broadcasted_iota(jnp.int32, shape, 1) // half - 2
        near = (kb - qb <= REACH) & (qb - kb <= REACH)
        near = near & (kb + 2 * f >= 0) & (kb + 2 * f < 2 * F)
        for i in range(heads):
            cols = slice(i * HEAD_SIZE, (i + 1) * HEAD_SIZE)
            scores = lax.dot_general(
                QB[:, cols], KB[s, :, cols], (((1,), (1,)), ((), ())), preferred_element_type=F32
            )
            raised = jnp.where(near, jnp.exp(scores * (1.0 / math.sqrt(HEAD_SIZE))), 0.0)
            weights = raised / jnp.sum(raised, axis=-1, keepdims=True)
            ATT[s, h, :, cols] = jnp.dot(
                weights.astype(BF16), VB[s, :, cols], preferred_element_type=F32
            ).astype(BF16)
        for step in range(1, H):
            send(ATT.at[s, h], ATT.at[s, h], t_send.at[s, step], t_recv.at[s, h], f, head_at(step))

    def attended_all(s):
        for step in range(1, H):
            g = head_at(step)
            arrived(ATT.at[s, g], t_recv.at[s, g])

    def advance(s, src):
        for n in range(chunks):
            cols = slice(n * NC, (n + 1) * NC)
            mixed = None
            for g in range(H):
                product = lax.dot_general(
                    ATT[s, g],
                    W[3, g, cols, :],
                    (((1,), (1,)), ((), ())),
                    preferred_element_type=F32,
                )
                product = product.astype(BF16).astype(F32)
                mixed = product if mixed is None else mixed + product
            for b in range(2):
                rows = slice(b * half, (b + 1) * half)
                base = src[rows, cols].astype(F32)
                gate = mod_ref[b * 3 + 2 : b * 3 + 3, cols]
                layer_out = base + gate * mixed[rows]
                following = (base + sigma_step(b) * layer_out).astype(BF16)
                if s == 1:
                    vel_ref[rows, cols] = layer_out.astype(BF16)
                    out_ref[rows, cols] = following
                elif b == 0:
                    NX[:, cols] = following
                else:
                    ZB[:half, cols] = following
            if s == 0:
                at = pl.ds(n * NC, NC)
                send(
                    NX.at[:, at],
                    ZB.at[pl.ds(half, half), at],
                    b_send.at[n],
                    b_recv.at[n],
                    f - 1,
                    h,
                    when=f > 0,
                )

    def second_state():
        for n in range(chunks):
            at = pl.ds(n * NC, NC)
            arrived(ZB.at[pl.ds(half, half), at], b_recv.at[n], when=f < F - 1)
        guarded(last, lambda: noise_own().wait())

    queue_own.wait()
    measure_rows(0, ZA)
    for m in range(M):
        w_along(m, 1)
        w_swap(m)
        if m:
            w_across(m - 1)
        if m + 3 < M:
            w_own(m + 3)
        for d in range(2, Z):
            w_along(m, d)
        w_heads(m)
        w_extra(m)
        if m == 2:
            table_own.wait()
            tables()
            modulate(0, ZA)
        if m == 3:
            w_last(0)
            w_last(1)
            project(0, 0)
        if m == 5:
            w_last(2)
            w_last(3)
            project(0, 1)
            keys(0)
    w_last(4)
    w_last(5)
    project(0, 2)
    values(0)
    queries(0)
    attend(0)
    w_across(M - 1)
    w_last(6)
    w_last(7)
    attended_all(0)
    advance(0, ZA)
    second_state()
    measure_rows(1, ZB)
    modulate(1, ZB)
    project(1, 0)
    project(1, 1)
    keys(1)
    project(1, 2)
    values(1)
    queries(1)
    attend(1)
    attended_all(1)
    advance(1, ZB)
    for when, action in pending:
        guarded(when, action)


def per_device(
    queue,
    noise_block,
    w_query,
    w_key,
    w_value,
    w_output,
    mod_table,
    sigma_table,
    timestep_index,
    block_position,
):
    F = lax.axis_size("frame")
    H = lax.axis_size("head")
    T, slab = queue.shape
    blocks = timestep_index.shape[0]
    half = T // blocks
    levels = mod_table.shape[0]
    R, inner = w_key.shape
    Z = F // 4
    zs = Z // H
    chunks = slab // 640
    freqs = 10000.0 ** (-np.arange(HEAD_SIZE // 2) / (HEAD_SIZE // 2))
    freqs = jnp.asarray(np.concatenate([freqs, freqs])[None, :].astype(np.float32))
    dma = pltpu.SemaphoreType.DMA
    vmem = pl.BlockSpec(memory_space=pltpu.VMEM)
    smem = pl.BlockSpec(memory_space=pltpu.SMEM)
    hbm = pl.BlockSpec(memory_space=pl.ANY)
    out = pltpu.VMEM((T, slab), BF16)
    return pl.pallas_call(
        functools.partial(kernel, F, H),
        out_shape=(out, out),
        in_specs=[hbm] * 7 + [vmem] + [smem] * 3,
        out_specs=(vmem, vmem),
        scratch_shapes=[
            pltpu.VMEM((4, H, slab, inner), BF16),
            pltpu.VMEM((8, Z, R // 2, inner), BF16),
            pltpu.VMEM((T, slab), BF16),
            pltpu.VMEM((T, slab), BF16),
            pltpu.VMEM((T, slab), BF16),
            pltpu.VMEM((half, slab), BF16),
            pltpu.VMEM((T, inner), BF16),
            pltpu.VMEM((2, 3 * T, inner), BF16),
            pltpu.VMEM((2, 3 * T, inner), BF16),
            pltpu.VMEM((2, H, T, inner), BF16),
            pltpu.VMEM((3, T, inner), F32),
            pltpu.VMEM((2, 3, H, T, inner), BF16),
            pltpu.VMEM((2, 3, H, T, inner), BF16),
            pltpu.VMEM((2, H, T, 128), F32),
            pltpu.VMEM((3, levels, slab), F32),
            pltpu.VMEM((blocks * 3, slab), F32),
            pltpu.VMEM((T, HEAD_SIZE), F32),
            pltpu.VMEM((T, HEAD_SIZE), F32),
            dma((3,)),
            dma((8, Z)),
            dma((8, Z)),
            dma((8, Z)),
            dma((8, Z)),
            dma((8, H, zs)),
            dma((8, H, zs)),
            dma((8, H, zs)),
            dma((8, H, zs, 2)),
            dma((8, H, zs, 2)),
            dma((8, zs)),
            dma((8,)),
            dma((8,)),
            dma((8,)),
            dma((chunks,)),
            dma((chunks,)),
            dma((2, 2)),
            dma((2, 2)),
            dma((2, 2)),
            dma((2, 2)),
            dma((2, H)),
            dma((2, H)),
            dma((2, 3, H)),
            dma((2, 3, H)),
            dma((2, H)),
            dma((2, H)),
        ],
        compiler_params=pltpu.CompilerParams(
            collective_id=0, has_side_effects=True, vmem_limit_bytes=62 * 1024 * 1024
        ),
        cost_estimate=pl.CostEstimate(
            flops=4 * T * H * slab * inner * 4, bytes_accessed=8 * R * inner * 2, transcendentals=0
        ),
    )(
        queue,
        noise_block,
        w_key,
        w_value,
        w_query,
        w_output.T,
        jnp.transpose(mod_table, (1, 0, 2)),
        freqs,
        sigma_table,
        timestep_index,
        block_position,
    )


def solution(mesh):
    in_specs = (
        P("frame", "head"),
        P(None, "head"),
        P("frame", "head"),
        P("frame", "head"),
        P("frame", "head"),
        P("head", "frame"),
        P(),
        P(),
        P("frame"),
        P("frame"),
    )
    out_specs = (P("frame", "head"), P("frame", "head"))
    return jax.shard_map(
        per_device, mesh=mesh, in_specs=in_specs, out_specs=out_specs, check_vma=False
    )
```
